32 devices in a mesh: fsdp: 16 (over z, x, core), dp: 2 (over y).
Axes of the slice: x: 2, y: 2, z: 4, core: 2. Of those that a mesh axis runs over, the one named last changes fastest.
Arguments:
- tokens: bfloat16 [32768, 512], P(('fsdp', 'dp')), may hold values from -6 to 6
- cotangent: bfloat16 [32768, 512], P(('fsdp', 'dp')), may hold values from -6 to 6
- key_valid: int32 [32], P(('fsdp', 'dp')), may hold values from 256 to 1024
- block_mask: int32 [32, 4, 4], P(('fsdp', 'dp')), may hold values 0 or 1
- row_owner: int32 [2, 16], replicated, may hold values from 0 to 15, each once within a row
- w_wide: float32 [2, 512, 4096], P(None, 'fsdp')
- w_down: float32 [2, 2048, 512], P(None, 'fsdp'), may hold values from -0.125 to 0.125
- gains: float32 [4, 512], replicated, may hold values from 0.5 to 1.5
- shifts: float32 [7, 512], replicated, may hold values from -3 to 3
- m_wide: float32 [2, 512, 4096], P(None, 'fsdp')
- v_wide: float32 [2, 512, 4096], P(None, 'fsdp')
- m_down: float32 [2, 2048, 512], P(None, 'fsdp')
- v_down: float32 [2, 2048, 512], P(None, 'fsdp')
- m_gain: float32 [4, 512], replicated
- v_gain: float32 [4, 512], replicated
- m_shift: float32 [7, 512], replicated
- v_shift: float32 [7, 512], replicated
Outputs:
- out_tokens: bfloat16 [32768, 512], P(('fsdp', 'dp'))
- grad_tokens: bfloat16 [32768, 512], P(('fsdp', 'dp'))
- new_wide: float32 [2, 512, 4096], P(None, 'fsdp')
- new_down: float32 [2, 2048, 512], P(None, 'fsdp')
- new_gains: float32 [4, 512], replicated
- new_shifts: float32 [7, 512], replicated
- first_wide: float32 [2, 512, 4096], P(None, 'fsdp')
- second_wide: float32 [2, 512, 4096], P(None, 'fsdp')
- first_down: float32 [2, 2048, 512], P(None, 'fsdp')
- second_down: float32 [2, 2048, 512], P(None, 'fsdp')
- first_gain: float32 [4, 512], replicated
- second_gain: float32 [4, 512], replicated
- first_shift: float32 [7, 512], replicated
- second_shift: float32 [7, 512], replicated
- wide_low: bfloat16 [2, 512, 4096], P(None, 'fsdp')
- down_low: bfloat16 [2, 2048, 512], P(None, 'fsdp')
The draws below stay inside these ranges and needn't reach their ends.
Inputs may be any that keep to these rules, and one draw needn't show every extreme that they name: `row_owner`: each row is a permutation of 0 to 15.
All inputs are finite; a program needn't handle non-finite values. No bound on the sum of `block_mask` on one device may be relied on, other than what follows from the above.
Results may differ from the reference program's by a relative error of at most 0.02.
Values may be sent and summed in bfloat16 or wider, within the bound.
No kernel may reach another device: no remote copies, remote signals or barrier semaphores. Data moves between devices by JAX's collectives and lax.ppermute only.
A program may use at most 192 MiB of HBM per device.

```python
import math
import jax
import jax.numpy as jnp
from jax import lax

D = 512
HEADS = 8
HEAD_DIM = 64
FF = 2048
LAYERS = 2
MEM_COLS = 64
QB_ROWS = 8
QB_COLS = 32
STEP = 5
TILE = 1024
NBLK = 4
TILES = 32
TOKENS = 32768
N_FSDP = 16


OUT_BOOST = 6.0


WIDE_GRAD = 0.3


DOWN_GRAD = 0.2


VECTOR_GRAD = 0.7


def scaled_first(key, array_shape, spread_scale):
    return spread_scale * jax.random.normal(key, array_shape, jnp.float32)


def scaled_second(key, array_shape, spread_scale):
    factor = jax.random.uniform(key, array_shape, jnp.float32, math.log(0.5), math.log(8.0))
    return spread_scale * spread_scale * jnp.exp(factor)


def draw_w_wide(key, part):
    key = jax.random.fold_in(key, 1)
    values = jax.random.normal(key, (LAYERS, D, 4 * D + FF), jnp.float32) / math.sqrt(D)
    columns = jnp.arange(4 * D + FF, dtype=jnp.int32)
    boost = jnp.where((columns >= 3 * D) & (columns < 4 * D), OUT_BOOST, 1.0)
    return values * boost


def draw_m_wide(key, part):
    key = jax.random.fold_in(key, 2)
    return scaled_first(key, (LAYERS, D, 4 * D + FF), WIDE_GRAD * math.sqrt(TOKENS))


def draw_v_wide(key, part):
    key = jax.random.fold_in(key, 3)
    return scaled_second(key, (LAYERS, D, 4 * D + FF), WIDE_GRAD * math.sqrt(TOKENS))


def draw_m_down(key, part):
    key = jax.random.fold_in(key, 4)
    return scaled_first(key, (LAYERS, FF, D), DOWN_GRAD * math.sqrt(TOKENS))


def draw_v_down(key, part):
    key = jax.random.fold_in(key, 5)
    return scaled_second(key, (LAYERS, FF, D), DOWN_GRAD * math.sqrt(TOKENS))


def draw_m_gain(key, part):
    key = jax.random.fold_in(key, 6)
    return scaled_first(key, (2 * LAYERS, D), VECTOR_GRAD * math.sqrt(TOKENS))


def draw_v_gain(key, part):
    key = jax.random.fold_in(key, 7)
    return scaled_second(key, (2 * LAYERS, D), VECTOR_GRAD * math.sqrt(TOKENS))


def draw_m_shift(key, part):
    key = jax.random.fold_in(key, 8)
    return scaled_first(key, (2 * LAYERS + 3, D), VECTOR_GRAD * math.sqrt(TOKENS))


def draw_v_shift(key, part):
    key = jax.random.fold_in(key, 9)
    return scaled_second(key, (2 * LAYERS + 3, D), VECTOR_GRAD * math.sqrt(TOKENS))


def place_ends(entries, rng, low, top_value):
    extent = entries.shape
    place = [jax.random.randint(jax.random.fold_in(rng, axis), (), 0, extent[axis]) for axis in range(len(extent))]
    entries = entries.at[tuple(place)].set(low)
    longest = extent.index(max(extent))
    place[longest] = (place[longest] + 1) % extent[longest]
    return entries.at[tuple(place)].set(top_value)


def steps_of(stream_key, extent, cuts, low, largest):
    level = 1.0
    for position, shards_of in cuts:
        heights = jax.random.uniform(jax.random.fold_in(jax.random.fold_in(stream_key, 6), position), (shards_of,), jnp.float32, low / len(cuts), largest / len(cuts))
        level = level * jnp.repeat(jnp.exp(heights), extent[position] // shards_of).reshape((-1,) + (1,) * (len(extent) - 1 - position))
    return level


def centred(stream_key, dims, deviation, bound, cuts=(), kind=jnp.bfloat16):
    values = deviation * jax.random.normal(stream_key, dims, jnp.float32)
    if cuts:
        values = values * steps_of(stream_key, dims, cuts, -0.22, 0.18)
    return jnp.clip(values, -bound, bound).astype(kind)


def setup_inputs(seed: int = 0) -> dict:
    key_list = jax.random.split(jax.random.key(seed), 18)
    tokens = centred(key_list[0], (TOKENS, D), 1.0, 6.0, ((0, 32),))
    cotangent = centred(key_list[1], (TOKENS, D), 1.0, 6.0, ((0, 32),))
    key_valid = place_ends(jax.random.randint(key_list[2], (TILES,), TILE // 4, TILE + 1), jax.random.fold_in(key_list[2], 1), TILE // 4, TILE).astype(jnp.int32)
    block_mask = place_ends((jax.random.randint(key_list[3], (TILES, NBLK, NBLK), 0, 2) < 1).astype(jnp.int32), jax.random.fold_in(key_list[3], 1), 0, 1)
    row_owner = jax.vmap(lambda own: jax.random.permutation(own, N_FSDP))(jax.random.split(key_list[4], LAYERS)).reshape((LAYERS, N_FSDP)).astype(jnp.int32)
    w_wide = draw_w_wide(jax.random.fold_in(key_list[17], 71), 0)
    w_down = centred(key_list[6], (LAYERS, FF, D), FF ** -0.5, 0.125, ((1, 16),), jnp.float32)
    gains = jnp.clip(1.0 + 0.1 * jax.random.normal(key_list[7], (2 * LAYERS, D), jnp.float32), 0.5, 1.5)
    shifts = centred(key_list[8], (2 * LAYERS + 3, D), 0.5, 3.0, (), jnp.float32)
    m_wide = draw_m_wide(jax.random.fold_in(key_list[17], 71), 0)
    v_wide = draw_v_wide(jax.random.fold_in(key_list[17], 71), 0)
    m_down = draw_m_down(jax.random.fold_in(key_list[17], 71), 0)
    v_down = draw_v_down(jax.random.fold_in(key_list[17], 71), 0)
    m_gain = draw_m_gain(jax.random.fold_in(key_list[17], 71), 0)
    v_gain = draw_v_gain(jax.random.fold_in(key_list[17], 71), 0)
    m_shift = draw_m_shift(jax.random.fold_in(key_list[17], 71), 0)
    v_shift = draw_v_shift(jax.random.fold_in(key_list[17], 71), 0)
    return {"tokens": tokens, "cotangent": cotangent, "key_valid": key_valid, "block_mask": block_mask, "row_owner": row_owner, "w_wide": w_wide, "w_down": w_down, "gains": gains, "shifts": shifts, "m_wide": m_wide, "v_wide": v_wide, "m_down": m_down, "v_down": v_down, "m_gain": m_gain, "v_gain": v_gain, "m_shift": m_shift, "v_shift": v_shift}


EXACT = lax.Precision.HIGHEST
NORM_EPS = 1e-05
SCORE_SCALE = 0.125
MASKED_SCORE = -1e+30
FIRST_DECAY = 0.5
SECOND_DECAY = 0.5
ADAM_EPS = 1e-08
WEIGHT_DECAY = 0.01
MATRIX_RATE = 0.02
VECTOR_RATE = 0.2

@jax.custom_vjp
def low(v):
    return lax.optimization_barrier(v.astype(jnp.bfloat16)).astype(jnp.float32)

@jax.custom_vjp
def low_back(v):
    return v

def low_keep(v):
    return (low(v), None)

def low_pass(kept, grad):
    return (grad,)

def back_keep(v):
    return (v, None)

def back_low(kept, grad):
    return (low(grad),)
low.defvjp(low_keep, low_pass)
low_back.defvjp(back_keep, back_low)

def matmul(left, right):
    return jnp.dot(left, right, precision=EXACT)

def layer_norm(residual, gain, shift):
    center = lax.optimization_barrier(jnp.mean(residual, axis=-1, keepdims=True))
    centered = residual - center
    variance = lax.optimization_barrier(jnp.mean(centered * centered, axis=-1, keepdims=True))
    return centered * lax.rsqrt(variance + NORM_EPS) * gain + shift

def visible_mask(valid_count, block_table):
    places = jnp.arange(TILE, dtype=jnp.int32)
    row_of = places // MEM_COLS
    col_of = places % MEM_COLS
    block_of = row_of // QB_ROWS * (MEM_COLS // QB_COLS) + col_of // QB_COLS
    onehot = (block_of[:, None] == jnp.arange(NBLK, dtype=jnp.int32)[None, :]).astype(jnp.float32)
    table = block_table.astype(jnp.float32)
    allowed = jnp.dot(jnp.dot(onehot, table, precision=EXACT), onehot.T, precision=EXACT) > 0.5
    causal = places[None, :] <= places[:, None]
    inside = places[None, :] < valid_count
    return allowed & causal & inside | (places[:, None] == places[None, :])

def channel_table(count):
    positions = jnp.arange(count, dtype=jnp.int32) % TILE % 3
    return (positions[:, None] == jnp.arange(3, dtype=jnp.int32)[None, :]).astype(jnp.float32)

def unpermute(stored, inverse):
    blocks = stored.reshape(N_FSDP, stored.shape[0] // N_FSDP, stored.shape[1])
    return blocks[inverse].reshape(stored.shape)

def tile_forward(params, inverse, tile_rows, valid_count, block_table):
    wide, down, gains, shifts = params
    mask = visible_mask(valid_count, block_table)
    state = tile_rows + matmul(channel_table(TILE), shifts[2 * LAYERS:])
    for level in range(LAYERS):
        weights_low = low(unpermute(wide[level], inverse[level]))
        down_weights = low(unpermute(down[level], inverse[level]))
        state_low = low(state)
        packed = low(low_back(matmul(state_low, weights_low[:, :3 * D])))
        split = packed.reshape(TILE, 3, HEADS, HEAD_DIM)
        scores = low_back(jnp.einsum('qhe,khe->hqk', split[:, 0], split[:, 1], precision=EXACT) * SCORE_SCALE)
        scores = jnp.where(mask[None], scores, MASKED_SCORE)
        top_score = lax.optimization_barrier(jnp.max(scores, axis=-1, keepdims=True))
        log_total = top_score + jnp.log(lax.optimization_barrier(jnp.sum(jnp.exp(scores - top_score), axis=-1, keepdims=True)))
        probs = low(jnp.exp(scores - log_total))
        mixed = jnp.einsum('hqk,khe->qhe', probs, split[:, 2], precision=EXACT).reshape(TILE, D)
        mixed = low(low_back(mixed))
        branch = low_back(matmul(mixed, weights_low[:, 3 * D:4 * D]))
        hidden = layer_norm(state + branch, gains[2 * level], shifts[2 * level])
        before = low_back(matmul(low(hidden), weights_low[:, 4 * D:]))
        active = low(jax.nn.gelu(before))
        result = low_back(matmul(active, down_weights))
        state = layer_norm(hidden + result, gains[2 * level + 1], shifts[2 * level + 1])
    return state

def adamw(weight, grad, first, second, rate):
    first_new = FIRST_DECAY * first + (1.0 - FIRST_DECAY) * grad
    second_new = SECOND_DECAY * second + (1.0 - SECOND_DECAY) * grad * grad
    first_fix = 1.0 - FIRST_DECAY ** STEP
    second_fix = 1.0 - SECOND_DECAY ** STEP
    update = first_new / first_fix / (jnp.sqrt(second_new / second_fix) + ADAM_EPS) + WEIGHT_DECAY * weight
    return (weight - rate * update, first_new, second_new)

def reference(tokens, cotangent, key_valid, block_mask, row_owner, w_wide, w_down, gains, shifts, m_wide, v_wide, m_down, v_down, m_gain, v_gain, m_shift, v_shift):
    inverse = jnp.argsort(row_owner, axis=-1).astype(jnp.int32)

    def forward(params, inputs):
        tiles = inputs.reshape(TILES, TILE, D)

        def one_tile(pieces):
            return tile_forward(params, inverse, pieces[0], pieces[1], pieces[2])
        outputs = lax.map(jax.checkpoint(one_tile), (tiles, key_valid, block_mask))
        return outputs.reshape(TOKENS, D)
    params = (w_wide, w_down, gains, shifts)
    output, pull = jax.vjp(forward, params, tokens.astype(jnp.float32))
    grads, grad_in = pull(cotangent.astype(jnp.float32))
    grad_wide, grad_down, grad_gain, grad_shift = grads
    new_wide, first_wide, second_wide = adamw(w_wide, grad_wide, m_wide, v_wide, MATRIX_RATE)
    new_down, first_down, second_down = adamw(w_down, grad_down, m_down, v_down, MATRIX_RATE)
    new_gains, first_gain, second_gain = adamw(gains, grad_gain, m_gain, v_gain, VECTOR_RATE)
    new_shifts, first_shift, second_shift = adamw(shifts, grad_shift, m_shift, v_shift, VECTOR_RATE)
    return (output.astype(jnp.bfloat16), grad_in.astype(jnp.bfloat16), new_wide, new_down, new_gains, new_shifts, first_wide, second_wide, first_down, second_down, first_gain, second_gain, first_shift, second_shift, new_wide.astype(jnp.bfloat16), new_down.astype(jnp.bfloat16))
```

```python
import functools

import jax
import jax.numpy as jnp
from jax import lax
from jax.experimental import pallas as pl
from jax.experimental.pallas import tpu as pltpu
from jax.sharding import PartitionSpec as P

D = 512
HEADS = 8
LAYERS = 2
STEP = 5
TILE = 1024
NBLK = 4
FF = 2048

NORM_EPS = 1e-05
MASKED_SCORE = -1e30
FIRST_DECAY = 0.5
SECOND_DECAY = 0.5
ADAM_EPS = 1e-08
WEIGHT_DECAY = 0.01
MATRIX_RATE = 0.02
VECTOR_RATE = 0.2

F32 = jnp.float32
BF16 = jnp.bfloat16
CH = 256
NCH = TILE // CH
KB = 16
WROWS = D // KB
DROWS = FF // KB
BLOCK_LANE = 24
SUM_LANE = 32
GELU_A = 0.7978845608028654
GELU_B = GELU_A * 0.044715
VMEM = pl.BlockSpec(memory_space=pltpu.VMEM)
SMEM = pl.BlockSpec(memory_space=pltpu.SMEM)
ANY = pl.BlockSpec(memory_space=pl.ANY)


def dn(a, b):
    return lax.dot_general(a, b, (((1,), (0,)), ((), ())), preferred_element_type=F32)


def nt(a, b):
    return lax.dot_general(a, b, (((1,), (1,)), ((), ())), preferred_element_type=F32)


def tn(a, b):
    return lax.dot_general(a, b, (((0,), (0,)), ((), ())), preferred_element_type=F32)


def rows(t):
    return slice(t * CH, (t + 1) * CH)


def normalize(r):
    center = jnp.mean(r, axis=-1, keepdims=True)
    centered = r - center
    variance = jnp.mean(centered * centered, axis=-1, keepdims=True)
    scale = lax.rsqrt(variance + NORM_EPS)
    return centered * scale, scale


def norm_back(dy, unit, scale, gain):
    du = dy * gain
    return scale * (
        du
        - jnp.mean(du, axis=-1, keepdims=True)
        - unit * jnp.mean(du * unit, axis=-1, keepdims=True)
    )


def load(bufs, place_ref, base, kind, vmem, sem):
    j = 0
    for ref, unit in bufs:
        for i in range(ref.shape[0]):
            start = pl.multiple_of(place_ref[kind, j], 16)
            if kind == 0:
                pltpu.make_async_copy(
                    ref.at[i, pl.ds(base, unit), :], vmem.at[pl.ds(start, unit), :], sem
                ).start()
            else:
                for g in range(4):
                    pltpu.make_async_copy(
                        ref.at[i, pl.ds(base, unit), pl.ds(g * D, D)],
                        vmem.at[pl.ds(pl.multiple_of(start + 32 * g, 16), unit), :],
                        sem,
                    ).start()
            j += 1


def unload(refs, place_ref, base, kind, vmem, sem):
    j = 0
    for ref in refs:
        for i in range(ref.shape[0]):
            start = pl.multiple_of(place_ref[kind, j], 16)
            if kind == 0:
                pltpu.make_async_copy(
                    vmem.at[pl.ds(start, WROWS), :], ref.at[i, pl.ds(base, WROWS), :], sem
                ).start()
            else:
                for g in range(4):
                    pltpu.make_async_copy(
                        vmem.at[pl.ds(pl.multiple_of(start + 32 * g, 16), WROWS), :],
                        ref.at[i, pl.ds(base, WROWS), pl.ds(g * D, D)],
                        sem,
                    ).start()
            j += 1


def whole(vmem, sem):
    pltpu.make_async_copy(vmem, vmem, sem).wait()


def lane_of(shape):
    return lax.broadcasted_iota(jnp.int32, shape, len(shape) - 1)


def attend_kernel(
    first, unit, count, place_ref, x_ref, vec_ref, kaug_ref, qone_ref, bias_ref, *rest,
):
    bufs = [(r, unit) for r in rest[:count]]
    xb_ref, qkv_ref, mixed_ref, lse_ref, r1_ref, w, sem = rest[count:]
    load(bufs, place_ref, 0, 0, w, sem)
    for t in range(NCH):
        x = x_ref[rows(t), :]
        if not first:
            x = normalize(x)[0] * vec_ref[0:1, :] + vec_ref[1:2, :]
        r1_ref[rows(t), :] = x
        xb_ref[rows(t), :] = x.astype(BF16)
    lse_ref[...] = jnp.zeros((TILE, 128), F32)
    whole(w, sem)
    for t in range(NCH):
        qkv_ref[rows(t), :] = dn(xb_ref[rows(t), :], w[:, : 3 * D]).astype(BF16)
    ones = jnp.ones((TILE, 128), BF16)
    lane = lane_of((CH, 128))

    def pair(hp, carry):
        at = pl.multiple_of(hp * 128, 128)
        keys = qkv_ref[:, pl.ds(D + at, 128)]
        full_keys = jnp.concatenate([keys, kaug_ref[...]], axis=1)
        full_values = jnp.concatenate([qkv_ref[:, pl.ds(2 * D + at, 128)], ones], axis=1)
        for t in range(NCH):
            queries = qkv_ref[rows(t), pl.ds(at, 128)] * jnp.asarray(0.125, BF16)
            outs = []
            for half in range(2):
                q = jnp.where((lane >= 64) == (half == 1), queries, jnp.zeros_like(queries))
                near = nt(q, keys[rows(t)]) + bias_ref[t]
                top = jnp.max(near, axis=-1, keepdims=True)
                if t:
                    far = nt(jnp.concatenate([q, qone_ref[rows(t), :]], axis=1), full_keys[: t * CH])
                    top = jnp.maximum(top, jnp.max(far, axis=-1, keepdims=True))
                    near = jnp.concatenate([far, near], axis=1)
                probs = jnp.exp(near - top).astype(BF16)
                o = dn(probs, full_values[: (t + 1) * CH])
                total = o[:, 128:]
                outs.append(o[:, :128] / total)
                here = ((lane & 7) == 2 * hp + half) & (lane < 24)
                lse_ref[rows(t), :] = jnp.where(here, top + jnp.log(total), lse_ref[rows(t), :])
            mixed_ref[rows(t), pl.ds(at, 128)] = jnp.where(lane < 64, outs[0], outs[1]).astype(BF16)
        return carry

    lax.fori_loop(0, HEADS // 2, pair, 0)
    for t in range(NCH):
        r1_ref[rows(t), :] += dn(mixed_ref[rows(t), :], w[:, 3 * D :])


def attend_back_kernel(
    first, unit, count, place_ref, gplace_ref, dr1_ref, mixed_ref, qkv_ref, lse_ref, xb_ref, kaug_ref,
    qone_ref, bias_ref, chan_ref, *rest,
):
    bufs = [(r, unit) for r in rest[:count]]
    dx_ref, keep_hbm, send_hbm, *rest = rest[count:]
    if first:
        dchan_ref, w, dm, extra, dq, dqkv, gw, sem, gsem = rest
    else:
        w, dm, extra, dq, dqkv, gw, sem, gsem = rest
    load(bufs, place_ref, 0, 0, w, sem)
    db = dr1_ref[...].astype(BF16)
    gw[:, 3 * D :] = tn(mixed_ref[...], db).astype(BF16)
    whole(w, sem)
    wide = lane_of((D, 128))
    feature = lax.broadcasted_iota(jnp.int32, (D, 128), 0)
    collect = jnp.where(
        ((feature >> 6) == (wide & 7)) & (wide >= SUM_LANE) & (wide < SUM_LANE + 24), 1.0, 0.0
    ).astype(BF16)
    lane = lane_of((CH, 128))
    group = (lane >> 3) & 3
    for t in range(NCH):
        d = nt(dr1_ref[rows(t), :].astype(BF16), w[:, 3 * D :]).astype(BF16)
        dm[rows(t), :] = d
        prod = d.astype(F32) * mixed_ref[rows(t), :].astype(F32)
        high = prod.astype(BF16)
        rest_ = (prod - high.astype(F32)).astype(BF16)
        v = lse_ref[rows(t), :] + dn(high, collect) + dn(rest_, collect)
        a = v.astype(BF16).astype(F32)
        b = (v - a).astype(BF16).astype(F32)
        c = v - a - b
        v = jnp.where(group == 0, a, jnp.where(group == 1, b, c))
        extra[rows(t), :] = (v + qone_ref[rows(t), :].astype(F32)).astype(BF16)
    one = lane_of((1, 128))
    alllane = lane_of((TILE, 128))

    def pair(hp, carry):
        at = pl.multiple_of(hp * 128, 128)
        queries = qkv_ref[:, pl.ds(at, 128)] * jnp.asarray(0.125, BF16)
        keys = qkv_ref[:, pl.ds(D + at, 128)]
        values = qkv_ref[:, pl.ds(2 * D + at, 128)]
        dmp = dm[:, pl.ds(at, 128)]
        full_q = jnp.concatenate([queries, extra[...]], axis=1)
        full_d = jnp.concatenate([dmp, extra[...]], axis=1)
        zero = jnp.zeros_like(queries)
        dks = [None] * NCH
        dvs = [None] * NCH
        for half in range(2):
            mine = (alllane >= 64) == (half == 1)
            h = 2 * hp + half
            q, k, v, g = (jnp.where(mine, a, zero) for a in (queries, keys, values, dmp))
            pick = ((one & 7) == h)
            sel_s = jnp.where(pick & (one < 24), -1.0, 0.0).astype(BF16)
            sel_d = jnp.where(pick & (one >= SUM_LANE) & (one < SUM_LANE + 24), -1.0, 0.0).astype(BF16)
            k8 = k * jnp.asarray(0.125, BF16)
            for c in range(NCH):
                near_k = jnp.concatenate([k[rows(c)], jnp.broadcast_to(sel_s, (CH, 128))], axis=1)
                s = nt(near_k, full_q[rows(c)]) + bias_ref[c]
                if c < NCH - 1:
                    far_k = jnp.concatenate([k[rows(c)], kaug_ref[rows(c), :] + sel_s], axis=1)
                    s = jnp.concatenate([s, nt(far_k, full_q[(c + 1) * CH :])], axis=1)
                p = jnp.exp(s)
                vf = jnp.concatenate([v[rows(c)], jnp.broadcast_to(sel_d, (CH, 128))], axis=1)
                ds = (p * nt(vf, full_d[c * CH :])).astype(BF16)
                dv = dn(p.astype(BF16), g[c * CH :])
                dk = dn(ds, q[c * CH :])
                dvs[c] = dv if half == 0 else dvs[c] + dv
                dks[c] = dk if half == 0 else dks[c] + dk
                part = tn(ds, k8[rows(c)])
                if half == 0 and c == 0:
                    dq[...] = part
                else:
                    dq[c * CH :, :] += part
        dqkv[:, pl.ds(at, 128)] = dq[...].astype(BF16)
        for c in range(NCH):
            dqkv[rows(c), pl.ds(D + at, 128)] = dks[c].astype(BF16)
            dqkv[rows(c), pl.ds(2 * D + at, 128)] = dvs[c].astype(BF16)
        return carry

    lax.fori_loop(0, HEADS // 2, pair, 0)
    gw[:, : 3 * D] = tn(xb_ref[...], dqkv[...]).astype(BF16)
    unload([keep_hbm, send_hbm], gplace_ref, 0, 0, gw, gsem)
    for t in range(NCH):
        dx = dr1_ref[rows(t), :] + nt(dqkv[rows(t), :], w[:, : 3 * D])
        dx_ref[rows(t), :] = dx.astype(dx_ref.dtype)
        if first:
            pick = chan_ref[:, rows(t)]
            a = dx.astype(BF16)
            b = (dx - a.astype(F32)).astype(BF16)
            c = (dx - a.astype(F32) - b.astype(F32)).astype(BF16)
            total = dn(pick, a) + dn(pick, b) + dn(pick, c)
            dchan_ref[...] = total if t == 0 else dchan_ref[...] + total
    whole(gw, gsem)


def forward_kernel(unit, base, count, place_ref, r1_ref, vec_ref, *rest):
    bufs = [(r, unit) for r in rest[:count]]
    r2_ref, w, wd, sem, dsem = rest[count:]
    load(bufs, place_ref, base, 0, w, sem)
    load(bufs, place_ref, base + unit, 1, wd, dsem)
    whole(w, sem)
    whole(wd, dsem)
    for t in range(NCH):
        h = normalize(r1_ref[rows(t), :])[0] * vec_ref[0:1, :] + vec_ref[1:2, :]
        hb = h.astype(BF16)
        back = h
        for c in range(FF // D):
            x = dn(hb, w[:, c * D : (c + 1) * D])
            half = 0.5 * x
            act = half + half * jnp.tanh(x * (GELU_A + GELU_B * (x * x)))
            back = back + dn(act.astype(BF16), wd[c * D : (c + 1) * D, :])
        r2_ref[rows(t), :] = back


def back_kernel(
    last, unit, base, count, place_ref, gplace_ref, dy_ref, r2_ref, r1_ref, vec_ref, *rest,
):
    bufs = [(r, unit) for r in rest[:count]]
    dr1_ref, g_hbm, dvec_ref, *rest = rest[count:]
    if last:
        out_ref, w, wd, dr2, db, hb, act, dpre, gw, gd, sem, dsem, gsem, gdsem = rest
    else:
        w, wd, dr2, db, hb, act, dpre, gw, gd, sem, dsem, gsem, gdsem = rest
    load(bufs, place_ref, base, 0, w, sem)
    load(bufs, place_ref, base + unit, 1, wd, dsem)
    dgain = jnp.zeros((1, D), F32)
    dshift = jnp.zeros((1, D), F32)
    for t in range(NCH):
        unit, scale = normalize(r2_ref[rows(t), :])
        dy = dy_ref[rows(t), :].astype(F32)
        if last:
            out_ref[rows(t), :] = (unit * vec_ref[2:3, :] + vec_ref[3:4, :]).astype(BF16)
        dgain += jnp.sum(dy * unit, axis=0, keepdims=True)
        dshift += jnp.sum(dy, axis=0, keepdims=True)
        dr = norm_back(dy, unit, scale, vec_ref[2:3, :])
        dr2[rows(t), :] = dr
        db[rows(t), :] = dr.astype(BF16)
        h = normalize(r1_ref[rows(t), :])[0] * vec_ref[0:1, :] + vec_ref[1:2, :]
        hb[rows(t), :] = h.astype(BF16)
    dvec_ref[2:3, :] = dgain
    dvec_ref[3:4, :] = dshift
    whole(w, sem)
    whole(wd, dsem)
    for t in range(NCH):
        for c in range(FF // D):
            cols = slice(c * D, (c + 1) * D)
            x = dn(hb[rows(t), :], w[:, cols])
            dact = nt(db[rows(t), :], wd[cols, :])
            half = 0.5 * x
            x2 = x * x
            th = jnp.tanh(x * (GELU_A + GELU_B * x2))
            act[rows(t), cols] = (half + half * th).astype(BF16)
            slope = (0.5 + 0.5 * th) + (half - half * (th * th)) * (GELU_A + 3 * GELU_B * x2)
            dp = (dact * slope).astype(BF16)
            dpre[rows(t), cols] = dp
            dr2[rows(t), :] += nt(dp, w[:, cols])
    for c in range(FF // D):
        cols = slice(c * D, (c + 1) * D)
        gd[cols, :] = tn(act[:, cols], db[...]).astype(BF16)
    unload([g_hbm], gplace_ref, WROWS, 1, gd, gdsem)
    for c in range(FF // D):
        cols = slice(c * D, (c + 1) * D)
        gw[:, cols] = tn(hb[...], dpre[:, cols]).astype(BF16)
    unload([g_hbm], gplace_ref, 0, 0, gw, gsem)
    dgain = jnp.zeros((1, D), F32)
    dshift = jnp.zeros((1, D), F32)
    for t in range(NCH):
        unit, scale = normalize(r1_ref[rows(t), :])
        dy = dr2[rows(t), :]
        dgain += jnp.sum(dy * unit, axis=0, keepdims=True)
        dshift += jnp.sum(dy, axis=0, keepdims=True)
        dr1_ref[rows(t), :] = norm_back(dy, unit, scale, vec_ref[0:1, :])
    dvec_ref[0:1, :] = dgain
    dvec_ref[1:2, :] = dshift
    whole(gd, gdsem)
    whole(gw, gsem)


def sds(shape, dtype=F32):
    return jax.ShapeDtypeStruct(shape, dtype)


def call(kernel, name, us, outs, in_specs, out_specs, scratch):
    return pl.pallas_call(
        kernel,
        out_shape=outs,
        in_specs=in_specs,
        out_specs=out_specs,
        scratch_shapes=scratch,
        compiler_params=pltpu.CompilerParams(vmem_limit_bytes=56 * 1024 * 1024),
        cost_estimate=pl.CostEstimate(flops=us * 1000000000, transcendentals=0, bytes_accessed=us * 3000000),
        name=name,
    )


DMA = pltpu.SemaphoreType.DMA


def attend(level, x, vec, masks, weights):
    kaug, qone, bias, _ = masks
    place, unit, _, bufs = weights
    return call(
        functools.partial(attend_kernel, level == 0, unit, len(bufs)),
        f"attend{level}",
        18,
        [sds((TILE, D), BF16), sds((TILE, 3 * D), BF16), sds((TILE, D), BF16), sds((TILE, 128)), sds((TILE, D))],
        [SMEM] + [VMEM] * 5 + [ANY] * len(bufs),
        [VMEM] * 5,
        [pltpu.VMEM((D, 4 * D), BF16), DMA],
    )(place, x, vec, kaug, qone, bias, *bufs)


def attend_back(level, dr1, mixed, qkv, lse, xb, masks, chan, weights, gplace):
    kaug, qone, _, bias = masks
    place, unit, _, bufs = weights
    first = level == 0
    grad = sds((KB // 2, WROWS, 4 * D), BF16)
    outs = [sds((TILE, D), BF16 if first else F32), grad, grad]
    specs = [VMEM, ANY, ANY]
    if first:
        outs.append(sds((8, D)))
        specs.append(VMEM)
    return call(
        functools.partial(attend_back_kernel, first, unit, len(bufs)),
        f"attend_back{level}",
        28,
        outs,
        [SMEM] * 2 + [VMEM] * 9 + [ANY] * len(bufs),
        specs,
        [
            pltpu.VMEM((D, 4 * D), BF16),
            pltpu.VMEM((TILE, D), BF16),
            pltpu.VMEM((TILE, 128), BF16),
            pltpu.VMEM((TILE, 128), F32),
            pltpu.VMEM((TILE, 3 * D), BF16),
            pltpu.VMEM((D, 4 * D), BF16),
            DMA,
            DMA,
        ],
    )(place, gplace, dr1, mixed, qkv, lse, xb, kaug, qone, bias, chan, *bufs)


def forward(level, r1, vec, weights):
    place, unit, base, bufs = weights
    return call(
        functools.partial(forward_kernel, unit, base, len(bufs)),
        f"forward{level}",
        12,
        sds((TILE, D)),
        [SMEM, VMEM, VMEM] + [ANY] * len(bufs),
        VMEM,
        [pltpu.VMEM((D, FF), BF16), pltpu.VMEM((FF, D), BF16), DMA, DMA],
    )(place, r1, vec, *bufs)


def back(level, dy, r2, r1, vec, weights, gplace):
    place, unit, base, bufs = weights
    last = level == LAYERS - 1
    outs = [sds((TILE, D)), sds((KB, 2 * WROWS, FF), BF16), sds((4, D))]
    specs = [VMEM, ANY, VMEM]
    if last:
        outs.append(sds((TILE, D), BF16))
        specs.append(VMEM)
    return call(
        functools.partial(back_kernel, last, unit, base, len(bufs)),
        f"back{level}",
        24,
        outs,
        [SMEM] * 2 + [VMEM] * 4 + [ANY] * len(bufs),
        specs,
        [
            pltpu.VMEM((D, FF), BF16),
            pltpu.VMEM((FF, D), BF16),
            pltpu.VMEM((TILE, D), F32),
            pltpu.VMEM((TILE, D), BF16),
            pltpu.VMEM((TILE, D), BF16),
            pltpu.VMEM((TILE, FF), BF16),
            pltpu.VMEM((TILE, FF), BF16),
            pltpu.VMEM((D, FF), BF16),
            pltpu.VMEM((FF, D), BF16),
            DMA,
            DMA,
            DMA,
            DMA,
        ],
    )(place, gplace, dy, r2, r1, vec, *bufs)


def mask_arrays(valid_count, table):
    places = jnp.arange(TILE, dtype=jnp.int32)
    block = (places >> 9) * 2 + ((places >> 5) & 1)
    member = block[:, None] == jnp.arange(NBLK, dtype=jnp.int32)[None, :]
    open_to = jnp.any(member[:, None, :] & (table[None] == 1), axis=-1) & (places < valid_count)[:, None]
    penalty = jnp.where(open_to, 0.0, MASKED_SCORE).astype(F32)
    pads = ((0, 0), (BLOCK_LANE, 128 - BLOCK_LANE - NBLK))
    kaug = jnp.pad(penalty, pads).astype(BF16)
    qone = jnp.pad(member.astype(F32), pads).astype(BF16)
    near = jnp.arange(CH, dtype=jnp.int32)
    visible = jnp.any(
        member.reshape(NCH, CH, 1, NBLK) & open_to.reshape(NCH, 1, CH, NBLK), axis=-1
    ) & (near[None, :] <= near[:, None])
    visible = visible | (near[None, :] == near[:, None])
    bias = jnp.where(visible, 0.0, MASKED_SCORE).astype(F32)
    return kaug, qone, bias, bias.transpose(0, 2, 1)


def adamw(weight, grad, first, second, rate):
    first_new = FIRST_DECAY * first + (1.0 - FIRST_DECAY) * grad
    second_new = SECOND_DECAY * second + (1.0 - SECOND_DECAY) * grad * grad
    first_fix = 1.0 - FIRST_DECAY**STEP
    second_fix = 1.0 - SECOND_DECAY**STEP
    update = (
        first_new / first_fix / (jnp.sqrt(second_new / second_fix) + ADAM_EPS)
        + WEIGHT_DECAY * weight
    )
    return (weight - rate * update, first_new, second_new)


def pick_rows(order, size):
    n = order.shape[0]
    place = (order[:, None] * size + jnp.arange(size, dtype=jnp.int32)[None, :]).reshape(-1)
    return (place[None, :] == jnp.arange(n * size, dtype=jnp.int32)[:, None]).astype(BF16)


def pack_down(down):
    lead = down.shape[:-2]
    return jnp.swapaxes(down.reshape(*lead, 4, WROWS, D), -3, -2).reshape(*lead, WROWS, FF)


def unpack_down(packed):
    lead = packed.shape[:-2]
    return jnp.swapaxes(packed.reshape(*lead, WROWS, 4, D), -3, -2).reshape(*lead, DROWS, D)


def swap(v, bit):
    n = lax.axis_size("fsdp")
    return lax.ppermute(v, "fsdp", [(i, i ^ bit) for i in range(n)])


def swap_dp(v):
    return lax.ppermute(v, "dp", [(0, 1), (1, 0)])


def add(a, b):
    return (a.astype(F32) + b.astype(F32)).astype(BF16)


def gather_near(shard):
    piece = jnp.concatenate([shard] + [swap(shard, 4 * k) for k in (1, 2, 3)], axis=0)
    piece = jnp.concatenate([piece, swap(piece, 2)], axis=0)
    other = swap_dp(piece)
    return [piece, other, swap(piece, 1), swap(other, 1)]


def halve(keep, send):
    part = add(keep, swap(send, 1))
    part = add(part[:4], swap(part[4:], 2))
    part = add(part[:2], swap(part[2:], 8))
    return add(part[:1], swap(part[1:], 4))[0]


def both(part):
    part = lax.reduce_precision(part.astype(F32), 8, 7)
    return part + swap_dp(part.astype(BF16)).astype(F32)


def vector_sum(v):
    def step(v, move):
        high = lax.reduce_precision(v, 8, 7)
        low = lax.reduce_precision(v - high, 8, 7)
        got = move(jnp.concatenate([high, low], axis=0).astype(BF16)).astype(F32)
        return (high + low) + (got[: v.shape[0]] + got[v.shape[0] :])
    v = step(v, lambda a: swap(a, 1))
    v = step(v, lambda a: swap(a, 2))
    v = step(v, lambda a: swap(a, 8))
    v = step(v, lambda a: swap(a, 4))
    return step(v, swap_dp)


def on_device(
    tokens, cotangent, key_valid, block_mask, row_owner, w_wide, w_down, gains, shifts,
    m_wide, v_wide, m_down, v_down, m_gain, v_gain, m_shift, v_shift,
):
    n = lax.axis_size("fsdp")
    direct = n == KB
    masks = mask_arrays(key_valid[0], block_mask[0])
    channel = jnp.arange(TILE, dtype=jnp.int32) % 3
    chan = (channel[None, :] == jnp.arange(8, dtype=jnp.int32)[:, None]).astype(BF16)
    embed = jnp.where(
        channel[:, None] == 0,
        shifts[2 * LAYERS],
        jnp.where(channel[:, None] == 1, shifts[2 * LAYERS + 1], shifts[2 * LAYERS + 2]),
    )
    x0 = tokens.astype(F32) + embed

    def places(order):
        return jnp.stack([order * WROWS, order * DROWS])

    natural = places(jnp.arange(KB, dtype=jnp.int32))
    if direct:
        me = lax.axis_index("fsdp")
        dp = lax.axis_index("dp")
        low = [w_wide[l].astype(BF16) for l in range(LAYERS)]
        low_down = [pack_down(w_down[l].astype(BF16)) for l in range(LAYERS)]
        mine = lambda a: lax.dynamic_slice_in_dim(a, dp * 16, 16, 0)[None]
        near_att = gather_near(mine(low[0][:, : 4 * D]))
        near_ff = gather_near(jnp.concatenate([mine(low[0][:, 4 * D :]), mine(low_down[0])], axis=1))
        packed = jnp.concatenate([low[1][:, : 4 * D], low[1][:, 4 * D :], low_down[1]], axis=0)
        far = lax.all_gather(packed, "fsdp", axis=0)
        kc, kd, kx, kz = (a.reshape(-1) for a in jnp.meshgrid(*(jnp.arange(s, dtype=jnp.int32) for s in (2, 2, 2, 4)), indexing="ij"))
        def owner_of(level, who):
            return jnp.sum(jnp.where(who[:, None] == jnp.arange(n, dtype=jnp.int32)[None, :], row_owner[level][None, :], 0), axis=1)
        own = owner_of(0, me ^ (kc + 2 * kx + 4 * kz))
        half = (dp ^ kd) * 16
        near_place = jnp.stack([own * WROWS + half, own * DROWS + half])
        relative = me ^ (jnp.arange(KB, dtype=jnp.int32) // 8 + 2 * ((jnp.arange(KB, dtype=jnp.int32) // 4) % 2) + 4 * (jnp.arange(KB, dtype=jnp.int32) % 4))
        att_weights = [(near_place, 16, 0, near_att), (places(row_owner[1]), 32, 0, [far])]
        ff_weights = [(near_place, 16, 0, near_ff), (places(row_owner[1]), 32, WROWS, [far])]
        ff_places = [places(row_owner[l]) for l in range(LAYERS)]
        att_places = [places(owner_of(l, relative)) for l in range(LAYERS)]
    else:
        att_weights = []
        for l in range(LAYERS):
            wide = lax.all_gather(w_wide[l].astype(BF16), "fsdp", axis=0, tiled=True)
            down = lax.all_gather(w_down[l].astype(BF16), "fsdp", axis=0, tiled=True)
            wide = dn(pick_rows(row_owner[l], D // n), wide).astype(BF16).reshape(KB, WROWS, 4 * D + FF)
            down = dn(pick_rows(row_owner[l], FF // n), down).astype(BF16).reshape(KB, DROWS, D)
            full = jnp.concatenate([wide[..., : 4 * D], wide[..., 4 * D :], pack_down(down)], axis=1)
            att_weights.append((natural, 32, 0, [full]))
        ff_weights = [(p, u, WROWS, b) for p, u, _, b in att_weights]
        ff_places = att_places = [natural] * LAYERS

    def sum_stored(level, full):
        pick = pick_rows(row_owner[level], full.shape[0] // n)
        part = lax.psum_scatter(tn(pick, full).astype(BF16), "fsdp", scatter_dimension=0, tiled=True)
        return both(part)

    def sum_ff(level, grad):
        if direct:
            part = both(lax.psum_scatter(grad, "fsdp", scatter_dimension=0))
            return part[:WROWS], unpack_down(part[WROWS:])
        up = sum_stored(level, grad[:, :WROWS].reshape(D, FF))
        return up, sum_stored(level, unpack_down(grad[:, WROWS:]).reshape(FF, D))

    def sum_att(level, keep, send):
        if direct:
            return both(halve(keep, send))
        return sum_stored(level, jnp.concatenate([keep, send], axis=0).reshape(D, 4 * D))

    vecs = [
        jnp.stack([gains[2 * l], shifts[2 * l], gains[2 * l + 1], shifts[2 * l + 1]])
        for l in range(LAYERS)
    ]
    state = x0
    saved = []
    for level in range(LAYERS):
        before = vecs[level - 1][2:4] if level else vecs[0][0:2]
        xb, qkv, mixed, lse, r1 = attend(level, state, before, masks, att_weights[level])
        state = forward(level, r1, vecs[level], ff_weights[level])
        saved.append((xb, qkv, mixed, lse, r1, state))
    dy = cotangent
    grad_gain = [None] * (2 * LAYERS)
    grad_shift = [None] * (2 * LAYERS)
    wide_grads = [None] * LAYERS
    down_grads = [None] * LAYERS
    for level in reversed(range(LAYERS)):
        xb, qkv, mixed, lse, r1, r2 = saved[level]
        dr1, g_ff, dvec, *out = back(level, dy, r2, r1, vecs[level], ff_weights[level], ff_places[level])
        if out:
            out_tokens = out[0]
        up, down_grads[level] = sum_ff(level, g_ff)
        dy, keep, send, *dchan = attend_back(
            level, dr1, mixed, qkv, lse, xb, masks, chan, att_weights[level], att_places[level]
        )
        wide_grads[level] = jnp.concatenate([sum_att(level, keep, send), up], axis=1)
        for i in range(2):
            grad_gain[2 * level + i] = dvec[2 * i]
            grad_shift[2 * level + i] = dvec[2 * i + 1]
    grad_tokens = dy
    vector_grad = jnp.concatenate(
        [jnp.stack(grad_gain), jnp.stack(grad_shift), dchan[0][:3]], axis=0
    )
    vector_grad = vector_sum(vector_grad) if direct else lax.psum(vector_grad, ("fsdp", "dp"))
    grad_gain, grad_shift = vector_grad[: 2 * LAYERS], vector_grad[2 * LAYERS :]
    grad_wide = jnp.stack(wide_grads)
    grad_down = jnp.stack(down_grads)
    new_wide, first_wide, second_wide = adamw(w_wide, grad_wide, m_wide, v_wide, MATRIX_RATE)
    new_down, first_down, second_down = adamw(w_down, grad_down, m_down, v_down, MATRIX_RATE)
    new_gains, first_gain, second_gain = adamw(gains, grad_gain, m_gain, v_gain, VECTOR_RATE)
    new_shifts, first_shift, second_shift = adamw(shifts, grad_shift, m_shift, v_shift, VECTOR_RATE)
    return (
        out_tokens,
        grad_tokens,
        new_wide,
        new_down,
        new_gains,
        new_shifts,
        first_wide,
        second_wide,
        first_down,
        second_down,
        first_gain,
        second_gain,
        first_shift,
        second_shift,
        new_wide.astype(BF16),
        new_down.astype(BF16),
    )


def solution(mesh):
    tile = P(("fsdp", "dp"))
    stored = P(None, "fsdp", None)
    in_specs = (tile, tile, tile, tile, P(), stored, stored, P(), P()) + (stored,) * 4 + (P(),) * 4
    out_specs = (tile, tile, stored, stored, P(), P()) + (stored,) * 4 + (P(),) * 4 + (stored,) * 2
    return jax.shard_map(
        on_device, mesh=mesh, in_specs=in_specs, out_specs=out_specs, check_vma=False
    )
```

```python
import functools

import jax
import jax.numpy as jnp
from jax import lax
from jax.experimental import pallas as pl
from jax.experimental.pallas import tpu as pltpu
from jax.sharding import PartitionSpec as P

D = 512
HEADS = 8
LAYERS = 2
STEP = 5
TILE = 1024
NBLK = 4
FF = 2048

NORM_EPS = 1e-05
MASKED_SCORE = -1e30
FIRST_DECAY = 0.5
SECOND_DECAY = 0.5
ADAM_EPS = 1e-08
WEIGHT_DECAY = 0.01
MATRIX_RATE = 0.02
VECTOR_RATE = 0.2

F32 = jnp.float32
BF16 = jnp.bfloat16
CH = 256
NCH = TILE // CH
KB = 16
WROWS = D // KB
DROWS = FF // KB
BLOCK_LANE = 24
SUM_LANE = 32
GELU_A = 0.7978845608028654
GELU_B = GELU_A * 0.044715
VMEM = pl.BlockSpec(memory_space=pltpu.VMEM)
SMEM = pl.BlockSpec(memory_space=pltpu.SMEM)
ANY = pl.BlockSpec(memory_space=pl.ANY)


def dn(a, b):
    return lax.dot_general(a, b, (((1,), (0,)), ((), ())), preferred_element_type=F32)


def nt(a, b):
    return lax.dot_general(a, b, (((1,), (1,)), ((), ())), preferred_element_type=F32)


def tn(a, b):
    return lax.dot_general(a, b, (((0,), (0,)), ((), ())), preferred_element_type=F32)


def rows(t):
    return slice(t * CH, (t + 1) * CH)


def normalize(r):
    center = jnp.mean(r, axis=-1, keepdims=True)
    centered = r - center
    variance = jnp.mean(centered * centered, axis=-1, keepdims=True)
    scale = lax.rsqrt(variance + NORM_EPS)
    return centered * scale, scale


def norm_back(dy, unit, scale, gain):
    du = dy * gain
    return scale * (
        du
        - jnp.mean(du, axis=-1, keepdims=True)
        - unit * jnp.mean(du * unit, axis=-1, keepdims=True)
    )


def load(refs, place_ref, parts, vmem, sem, down=False):
    for first, count, kind, unit, source, width, target in parts:
        j = 0
        for ref in refs[first : first + count]:
            for i in range(ref.shape[0]):
                start = pl.multiple_of(place_ref[kind, j], 16)
                j += 1
                for g in range(4 if down else 1):
                    columns = pl.ds(source + g * D, D) if down else pl.ds(source, width)
                    at = pl.ds(pl.multiple_of(start + 32 * g, 16), unit)
                    to = pl.ds(0, D) if down else pl.ds(target, width)
                    pltpu.make_async_copy(ref.at[i, :, columns], vmem.at[at, to], sem).start()


def unload(refs, place_ref, base, kind, vmem, sem):
    j = 0
    for ref in refs:
        for i in range(ref.shape[0]):
            start = pl.multiple_of(place_ref[kind, j], 16)
            j += 1
            for g in range(4 if kind else 1):
                at = pl.ds(pl.multiple_of(start + 32 * g, 16), WROWS)
                to = ref.at[i, :, pl.ds(base + g * D, D)] if kind else ref.at[i, :, pl.ds(base, vmem.shape[1])]
                pltpu.make_async_copy(vmem.at[at, :], to, sem).start()


def whole(vmem, sem):
    pltpu.make_async_copy(vmem, vmem, sem).wait()


def lane_of(shape):
    return lax.broadcasted_iota(jnp.int32, shape, len(shape) - 1)


def attend_kernel(
    first, parts, count, place_ref, x_ref, vec_ref, kaug_ref, qone_ref, bias_ref, *rest,
):
    refs = rest[:count]
    xb_ref, qkv_ref, mixed_ref, lse_ref, state_ref, w, sem = rest[count:]
    load(refs, place_ref, parts["qkv"], w, sem)
    for t in range(NCH):
        x = x_ref[rows(t), :]
        if not first:
            x = normalize(x)[0] * vec_ref[0:1, :] + vec_ref[1:2, :]
        state_ref[rows(t), :] = x
        xb_ref[rows(t), :] = x.astype(BF16)
    lse_ref[...] = jnp.zeros((TILE, 128), F32)
    whole(w, sem)
    for t in range(NCH):
        qkv_ref[rows(t), :] = dn(xb_ref[rows(t), :], w[...]).astype(BF16)
    ones = jnp.ones((TILE, 128), BF16)
    lane = lane_of((CH, 128))

    def pair(hp, carry):
        at = pl.multiple_of(hp * 128, 128)
        keys = qkv_ref[:, pl.ds(D + at, 128)]
        full_keys = jnp.concatenate([keys, kaug_ref[...]], axis=1)
        full_values = jnp.concatenate([qkv_ref[:, pl.ds(2 * D + at, 128)], ones], axis=1)
        for t in range(NCH):
            queries = qkv_ref[rows(t), pl.ds(at, 128)] * jnp.asarray(0.125, BF16)
            outs = []
            for half in range(2):
                q = jnp.where((lane >= 64) == (half == 1), queries, jnp.zeros_like(queries))
                near = nt(q, keys[rows(t)]) + bias_ref[t]
                top = jnp.max(near, axis=-1, keepdims=True)
                if t:
                    far = nt(jnp.concatenate([q, qone_ref[rows(t), :]], axis=1), full_keys[: t * CH])
                    top = jnp.maximum(top, jnp.max(far, axis=-1, keepdims=True))
                    near = jnp.concatenate([far, near], axis=1)
                probs = jnp.exp(near - top).astype(BF16)
                o = dn(probs, full_values[: (t + 1) * CH])
                total = o[:, 128:]
                outs.append(o[:, :128] / total)
                here = ((lane & 7) == 2 * hp + half) & (lane < 24)
                lse_ref[rows(t), :] = jnp.where(here, top + jnp.log(total), lse_ref[rows(t), :])
            mixed_ref[rows(t), pl.ds(at, 128)] = jnp.where(lane < 64, outs[0], outs[1]).astype(BF16)
        return carry

    lax.fori_loop(0, HEADS // 2, pair, 0)


def before_pairs(dr1_ref, mixed_ref, lse_ref, qone_ref, wo, dm, extra):
    wide = lane_of((D, 128))
    feature = lax.broadcasted_iota(jnp.int32, (D, 128), 0)
    collect = jnp.where(
        ((feature >> 6) == (wide & 7)) & (wide >= SUM_LANE) & (wide < SUM_LANE + 24), 1.0, 0.0
    ).astype(BF16)
    group = (lane_of((CH, 128)) >> 3) & 3
    for t in range(NCH):
        d = nt(dr1_ref[rows(t), :].astype(BF16), wo[...]).astype(BF16)
        dm[rows(t), :] = d
        prod = d.astype(F32) * mixed_ref[rows(t), :].astype(F32)
        high = prod.astype(BF16)
        low = (prod - high.astype(F32)).astype(BF16)
        v = lse_ref[rows(t), :] + dn(high, collect) + dn(low, collect)
        a = v.astype(BF16).astype(F32)
        b = (v - a).astype(BF16).astype(F32)
        c = v - a - b
        v = jnp.where(group == 0, a, jnp.where(group == 1, b, c))
        extra[rows(t), :] = (v + qone_ref[rows(t), :].astype(F32)).astype(BF16)


def back_pairs(start, count, qkv_ref, dm, extra, kaug_ref, bias_ref, dq, dqkv):
    one = lane_of((1, 128))
    alllane = lane_of((TILE, 128))
    width = count * 128

    def pair(i, carry):
        hp = i + start
        at = pl.multiple_of(hp * 128, 128)
        to = pl.multiple_of(i * 128, 128)
        queries = qkv_ref[:, pl.ds(at, 128)] * jnp.asarray(0.125, BF16)
        keys = qkv_ref[:, pl.ds(D + at, 128)]
        values = qkv_ref[:, pl.ds(2 * D + at, 128)]
        dmp = dm[:, pl.ds(at, 128)]
        full_q = jnp.concatenate([queries, extra[...]], axis=1)
        full_d = jnp.concatenate([dmp, extra[...]], axis=1)
        zero = jnp.zeros_like(queries)
        dks = [None] * NCH
        dvs = [None] * NCH
        for half in range(2):
            mine = (alllane >= 64) == (half == 1)
            h = 2 * hp + half
            q, k, v, g = (jnp.where(mine, a, zero) for a in (queries, keys, values, dmp))
            pick = (one & 7) == h
            sel_s = jnp.where(pick & (one < 24), -1.0, 0.0).astype(BF16)
            sel_d = jnp.where(pick & (one >= SUM_LANE) & (one < SUM_LANE + 24), -1.0, 0.0).astype(BF16)
            k8 = k * jnp.asarray(0.125, BF16)
            for c in range(NCH):
                near_k = jnp.concatenate([k[rows(c)], jnp.broadcast_to(sel_s, (CH, 128))], axis=1)
                s = nt(near_k, full_q[rows(c)]) + bias_ref[c]
                if c < NCH - 1:
                    far_k = jnp.concatenate([k[rows(c)], kaug_ref[rows(c), :] + sel_s], axis=1)
                    s = jnp.concatenate([s, nt(far_k, full_q[(c + 1) * CH :])], axis=1)
                p = jnp.exp(s)
                vf = jnp.concatenate([v[rows(c)], jnp.broadcast_to(sel_d, (CH, 128))], axis=1)
                ds = (p * nt(vf, full_d[c * CH :])).astype(BF16)
                dv = dn(p.astype(BF16), g[c * CH :])
                dk = dn(ds, q[c * CH :])
                dvs[c] = dv if half == 0 else dvs[c] + dv
                dks[c] = dk if half == 0 else dks[c] + dk
                part = tn(ds, k8[rows(c)])
                if half == 0 and c == 0:
                    dq[...] = part
                else:
                    dq[c * CH :, :] += part
        dqkv[:, pl.ds(to, 128)] = dq[...].astype(BF16)
        for c in range(NCH):
            dqkv[rows(c), pl.ds(width + to, 128)] = dks[c].astype(BF16)
            dqkv[rows(c), pl.ds(2 * width + to, 128)] = dvs[c].astype(BF16)
        return carry

    lax.fori_loop(0, count, pair, 0)


def attend_back_kernel(
    parts, count, place_ref, gplace_ref, dr1_ref, mixed_ref, qkv_ref, lse_ref, xb_ref, kaug_ref,
    qone_ref, bias_ref, *rest,
):
    refs = rest[:count]
    dx_ref, *g_hbm, w, wo, dm, extra, dq, dqkv, gw, sem, osem, gsem = rest[count:]
    load(refs, place_ref, parts["wo"], wo, osem)
    load(refs, place_ref, parts["qkv"], w, sem)
    gw[:, 3 * D :] = tn(mixed_ref[...], dr1_ref[...].astype(BF16)).astype(BF16)
    whole(wo, osem)
    before_pairs(dr1_ref, mixed_ref, lse_ref, qone_ref, wo, dm, extra)
    back_pairs(0, HEADS // 2, qkv_ref, dm, extra, kaug_ref, bias_ref, dq, dqkv)
    gw[:, : 3 * D] = tn(xb_ref[...], dqkv[...]).astype(BF16)
    unload(g_hbm, gplace_ref, 0, 0, gw, gsem)
    whole(w, sem)
    for t in range(NCH):
        dx_ref[rows(t), :] = dr1_ref[rows(t), :] + nt(dqkv[rows(t), :], w[...])
    whole(gw, gsem)


def left_kernel(
    parts, count, place_ref, gplace_ref, dr1_ref, mixed_ref, qkv_ref, lse_ref, xb_ref, kaug_ref,
    qone_ref, bias_ref, *rest,
):
    refs = rest[:count]
    dm, extra, dqkv, keep_hbm, send_hbm, wo, dq, gw, osem, gsem = rest[count:]
    load(refs, place_ref, parts["wo"], wo, osem)
    gw[:, 3 * D // 2 :] = tn(mixed_ref[...], dr1_ref[...].astype(BF16)).astype(BF16)
    whole(wo, osem)
    before_pairs(dr1_ref, mixed_ref, lse_ref, qone_ref, wo, dm, extra)
    back_pairs(0, HEADS // 4, qkv_ref, dm, extra, kaug_ref, bias_ref, dq, dqkv)
    gw[:, : 3 * D // 2] = tn(xb_ref[...], dqkv[...]).astype(BF16)
    unload([keep_hbm, send_hbm], gplace_ref, 0, 0, gw, gsem)
    whole(gw, gsem)


def right_kernel(
    gplace_ref, qkv_ref, dm, extra, xb_ref, kaug_ref, bias_ref, dqkv, keep_hbm, send_hbm, dq, gw, gsem,
):
    back_pairs(HEADS // 4, HEADS // 4, qkv_ref, dm, extra, kaug_ref, bias_ref, dq, dqkv)
    gw[...] = tn(xb_ref[...], dqkv[...]).astype(BF16)
    unload([keep_hbm, send_hbm], gplace_ref, 0, 0, gw, gsem)
    whole(gw, gsem)


def input_kernel(parts, count, place_ref, dr1_ref, left_ref, right_ref, chan_ref, *rest):
    refs = rest[:count]
    dx_ref, dchan_ref, w, sem = rest[count:]
    load(refs, place_ref, parts["qkv"], w, sem)
    whole(w, sem)
    half = D // 2
    for t in range(NCH):
        grads = [
            ref[rows(t), i * half : (i + 1) * half] for i in range(3) for ref in (left_ref, right_ref)
        ]
        dx = dr1_ref[rows(t), :] + nt(jnp.concatenate(grads, axis=1), w[...])
        dx_ref[rows(t), :] = dx.astype(BF16)
        pick = chan_ref[:, rows(t)]
        a = dx.astype(BF16)
        b = (dx - a.astype(F32)).astype(BF16)
        c = (dx - a.astype(F32) - b.astype(F32)).astype(BF16)
        total = dn(pick, a) + dn(pick, b) + dn(pick, c)
        dchan_ref[...] = total if t == 0 else dchan_ref[...] + total


def forward_kernel(parts, count, place_ref, x_ref, mixed_ref, vec_ref, *rest):
    refs = rest[:count]
    r1_ref, r2_ref, wo, w, wd, osem, sem, dsem = rest[count:]
    load(refs, place_ref, parts["wo"], wo, osem)
    load(refs, place_ref, parts["up"], w, sem)
    load(refs, place_ref, parts["down"], wd, dsem, True)
    whole(wo, osem)
    for t in range(NCH):
        r1 = x_ref[rows(t), :] + dn(mixed_ref[rows(t), :], wo[...])
        r1_ref[rows(t), :] = r1
        r2_ref[rows(t), :] = normalize(r1)[0] * vec_ref[0:1, :] + vec_ref[1:2, :]
    whole(w, sem)
    whole(wd, dsem)
    for t in range(NCH):
        back = r2_ref[rows(t), :]
        hb = back.astype(BF16)
        for c in range(FF // D):
            x = dn(hb, w[:, c * D : (c + 1) * D])
            half = 0.5 * x
            act = half + half * jnp.tanh(x * (GELU_A + GELU_B * (x * x)))
            back = back + dn(act.astype(BF16), wd[c * D : (c + 1) * D, :])
        r2_ref[rows(t), :] = back


def back_kernel(
    last, parts, count, gcount, place_ref, gplace_ref, dy_ref, r2_ref, r1_ref, vec_ref, *rest,
):
    refs = rest[:count]
    g_hbm = rest[count : count + gcount]
    dr1_ref, dvec_ref, *rest = rest[count + gcount :]
    if last:
        out_ref, w, wd, dr2, db, hb, act, dpre, gw, gd, sem, dsem, gsem, gdsem = rest
    else:
        w, wd, dr2, db, hb, act, dpre, gw, gd, sem, dsem, gsem, gdsem = rest
    load(refs, place_ref, parts["up"], w, sem)
    load(refs, place_ref, parts["down"], wd, dsem, True)
    dgain = jnp.zeros((1, D), F32)
    dshift = jnp.zeros((1, D), F32)
    for t in range(NCH):
        unit, scale = normalize(r2_ref[rows(t), :])
        dy = dy_ref[rows(t), :].astype(F32)
        if last:
            out_ref[rows(t), :] = (unit * vec_ref[2:3, :] + vec_ref[3:4, :]).astype(BF16)
        dgain += jnp.sum(dy * unit, axis=0, keepdims=True)
        dshift += jnp.sum(dy, axis=0, keepdims=True)
        dr = norm_back(dy, unit, scale, vec_ref[2:3, :])
        dr2[rows(t), :] = dr
        db[rows(t), :] = dr.astype(BF16)
        h = normalize(r1_ref[rows(t), :])[0] * vec_ref[0:1, :] + vec_ref[1:2, :]
        hb[rows(t), :] = h.astype(BF16)
    dvec_ref[2:3, :] = dgain
    dvec_ref[3:4, :] = dshift
    whole(w, sem)
    whole(wd, dsem)
    for t in range(NCH):
        for c in range(FF // D):
            cols = slice(c * D, (c + 1) * D)
            x = dn(hb[rows(t), :], w[:, cols])
            dact = nt(db[rows(t), :], wd[cols, :])
            half = 0.5 * x
            x2 = x * x
            th = jnp.tanh(x * (GELU_A + GELU_B * x2))
            act[rows(t), cols] = (half + half * th).astype(BF16)
            slope = (0.5 + 0.5 * th) + (half - half * (th * th)) * (GELU_A + 3 * GELU_B * x2)
            dp = (dact * slope).astype(BF16)
            dpre[rows(t), cols] = dp
            dr2[rows(t), :] += nt(dp, w[:, cols])
    for c in range(FF // D):
        cols = slice(c * D, (c + 1) * D)
        gd[cols, :] = tn(act[:, cols], db[...]).astype(BF16)
    unload(g_hbm, gplace_ref, FF, 1, gd, gdsem)
    for c in range(FF // D):
        cols = slice(c * D, (c + 1) * D)
        gw[:, cols] = tn(hb[...], dpre[:, cols]).astype(BF16)
    unload(g_hbm, gplace_ref, 0, 0, gw, gsem)
    dgain = jnp.zeros((1, D), F32)
    dshift = jnp.zeros((1, D), F32)
    for t in range(NCH):
        unit, scale = normalize(r1_ref[rows(t), :])
        dy = dr2[rows(t), :]
        dgain += jnp.sum(dy * unit, axis=0, keepdims=True)
        dshift += jnp.sum(dy, axis=0, keepdims=True)
        dr1_ref[rows(t), :] = norm_back(dy, unit, scale, vec_ref[0:1, :])
    dvec_ref[0:1, :] = dgain
    dvec_ref[1:2, :] = dshift
    whole(gd, gdsem)
    whole(gw, gsem)


def sds(shape, dtype=F32):
    return jax.ShapeDtypeStruct(shape, dtype)


def call(kernel, name, us, outs, in_specs, out_specs, scratch):
    return pl.pallas_call(
        kernel,
        out_shape=outs,
        in_specs=in_specs,
        out_specs=out_specs,
        scratch_shapes=scratch,
        compiler_params=pltpu.CompilerParams(vmem_limit_bytes=56 * 1024 * 1024),
        cost_estimate=pl.CostEstimate(flops=us * 400000000, transcendentals=0, bytes_accessed=us * 1200000),
        name=name,
    )


DMA = pltpu.SemaphoreType.DMA


def attend(level, x, vec, masks, weights):
    kaug, qone, bias, _ = masks
    place, parts, bufs = weights
    return call(
        functools.partial(attend_kernel, level == 0, parts, len(bufs)),
        f"attend{level}",
        18,
        [sds((TILE, D), BF16), sds((TILE, 3 * D), BF16), sds((TILE, D), BF16), sds((TILE, 128)), sds((TILE, D))],
        [SMEM] + [VMEM] * 5 + [ANY] * len(bufs),
        [VMEM] * 5,
        [pltpu.VMEM((D, 3 * D), BF16), DMA],
    )(place, x, vec, kaug, qone, bias, *bufs)


def grad_pair(columns):
    return [sds((KB // 2, WROWS, columns), BF16)] * 2


def attend_back(dr1, kept, masks, weights, gplace):
    kaug, qone, _, bias = masks
    place, parts, bufs = weights
    xb, qkv, mixed, lse = kept
    return call(
        functools.partial(attend_back_kernel, parts, len(bufs)),
        "attend_back",
        28,
        [sds((TILE, D))] + grad_pair(4 * D),
        [SMEM] * 2 + [VMEM] * 8 + [ANY] * len(bufs),
        [VMEM, ANY, ANY],
        [
            pltpu.VMEM((D, 3 * D), BF16),
            pltpu.VMEM((D, D), BF16),
            pltpu.VMEM((TILE, D), BF16),
            pltpu.VMEM((TILE, 128), BF16),
            pltpu.VMEM((TILE, 128), F32),
            pltpu.VMEM((TILE, 3 * D), BF16),
            pltpu.VMEM((D, 4 * D), BF16),
            DMA,
            DMA,
            DMA,
        ],
    )(place, gplace, dr1, mixed, qkv, lse, xb, kaug, qone, bias, *bufs)


def attend_left(dr1, kept, masks, weights, gplace):
    kaug, qone, _, bias = masks
    place, parts, bufs = weights
    xb, qkv, mixed, lse = kept
    return call(
        functools.partial(left_kernel, parts, len(bufs)),
        "attend_left",
        17,
        [sds((TILE, D), BF16), sds((TILE, 128), BF16), sds((TILE, 3 * D // 2), BF16)] + grad_pair(5 * D // 2),
        [SMEM] * 2 + [VMEM] * 8 + [ANY] * len(bufs),
        [VMEM, VMEM, VMEM, ANY, ANY],
        [
            pltpu.VMEM((D, D), BF16),
            pltpu.VMEM((TILE, 128), F32),
            pltpu.VMEM((D, 5 * D // 2), BF16),
            DMA,
            DMA,
        ],
    )(place, gplace, dr1, mixed, qkv, lse, xb, kaug, qone, bias, *bufs)


def attend_right(dm, extra, kept, masks, gplace):
    kaug, _, _, bias = masks
    xb, qkv = kept[:2]
    return call(
        right_kernel,
        "attend_right",
        14,
        [sds((TILE, 3 * D // 2), BF16)] + grad_pair(3 * D // 2),
        [SMEM] + [VMEM] * 6,
        [VMEM, ANY, ANY],
        [pltpu.VMEM((TILE, 128), F32), pltpu.VMEM((D, 3 * D // 2), BF16), DMA],
    )(gplace, qkv, dm, extra, xb, kaug, bias)


def input_grad(dr1, left, right, chan, weights):
    place, parts, bufs = weights
    return call(
        functools.partial(input_kernel, parts, len(bufs)),
        "input_grad",
        30,
        [sds((TILE, D), BF16), sds((8, D))],
        [SMEM] + [VMEM] * 4 + [ANY] * len(bufs),
        [VMEM, VMEM],
        [pltpu.VMEM((D, 3 * D), BF16), DMA],
    )(place, dr1, left, right, chan, *bufs)


def forward(level, x, mixed, vec, weights):
    place, parts, bufs = weights
    return call(
        functools.partial(forward_kernel, parts, len(bufs)),
        f"forward{level}",
        13,
        [sds((TILE, D)), sds((TILE, D))],
        [SMEM, VMEM, VMEM, VMEM] + [ANY] * len(bufs),
        [VMEM, VMEM],
        [pltpu.VMEM((D, D), BF16), pltpu.VMEM((D, FF), BF16), pltpu.VMEM((FF, D), BF16), DMA, DMA, DMA],
    )(place, x, mixed, vec, *bufs)


def back(level, dy, r2, r1, vec, weights, gplace, split):
    place, parts, bufs = weights
    last = level == LAYERS - 1
    grads = [sds((KB // split, WROWS, 2 * FF), BF16)] * split
    outs = grads + [sds((TILE, D)), sds((4, D))]
    specs = [ANY] * split + [VMEM, VMEM]
    if last:
        outs.append(sds((TILE, D), BF16))
        specs.append(VMEM)
    got = call(
        functools.partial(back_kernel, last, parts, len(bufs), split),
        f"back{level}",
        24,
        outs,
        [SMEM] * 2 + [VMEM] * 4 + [ANY] * len(bufs),
        specs,
        [
            pltpu.VMEM((D, FF), BF16),
            pltpu.VMEM((FF, D), BF16),
            pltpu.VMEM((TILE, D), F32),
            pltpu.VMEM((TILE, D), BF16),
            pltpu.VMEM((TILE, D), BF16),
            pltpu.VMEM((TILE, FF), BF16),
            pltpu.VMEM((TILE, FF), BF16),
            pltpu.VMEM((D, FF), BF16),
            pltpu.VMEM((FF, D), BF16),
            DMA,
            DMA,
            DMA,
            DMA,
        ],
    )(place, gplace, dy, r2, r1, vec, *bufs)
    return got[:split], *got[split:]


def mask_arrays(valid_count, table):
    places = jnp.arange(TILE, dtype=jnp.int32)
    block = (places >> 9) * 2 + ((places >> 5) & 1)
    member = block[:, None] == jnp.arange(NBLK, dtype=jnp.int32)[None, :]
    open_to = jnp.any(member[:, None, :] & (table[None] == 1), axis=-1) & (places < valid_count)[:, None]
    penalty = jnp.where(open_to, 0.0, MASKED_SCORE).astype(F32)
    pads = ((0, 0), (BLOCK_LANE, 128 - BLOCK_LANE - NBLK))
    kaug = jnp.pad(penalty, pads).astype(BF16)
    qone = jnp.pad(member.astype(F32), pads).astype(BF16)
    near = jnp.arange(CH, dtype=jnp.int32)
    visible = jnp.any(
        member.reshape(NCH, CH, 1, NBLK) & open_to.reshape(NCH, 1, CH, NBLK), axis=-1
    ) & (near[None, :] <= near[:, None])
    visible = visible | (near[None, :] == near[:, None])
    bias = jnp.where(visible, 0.0, MASKED_SCORE).astype(F32)
    return kaug, qone, bias, bias.transpose(0, 2, 1)


def adamw(weight, grad, first, second, rate):
    first_new = FIRST_DECAY * first + (1.0 - FIRST_DECAY) * grad
    second_new = SECOND_DECAY * second + (1.0 - SECOND_DECAY) * grad * grad
    first_fix = 1.0 - FIRST_DECAY**STEP
    second_fix = 1.0 - SECOND_DECAY**STEP
    update = (
        first_new / first_fix / (jnp.sqrt(second_new / second_fix) + ADAM_EPS)
        + WEIGHT_DECAY * weight
    )
    return (weight - rate * update, first_new, second_new)


def pick_rows(order, size):
    n = order.shape[0]
    place = (order[:, None] * size + jnp.arange(size, dtype=jnp.int32)[None, :]).reshape(-1)
    return (place[None, :] == jnp.arange(n * size, dtype=jnp.int32)[:, None]).astype(BF16)


def pack_down(down):
    lead = down.shape[:-2]
    return jnp.swapaxes(down.reshape(*lead, 4, WROWS, D), -3, -2).reshape(*lead, WROWS, FF)


def unpack_down(packed):
    lead = packed.shape[:-2]
    return jnp.swapaxes(packed.reshape(*lead, WROWS, 4, D), -3, -2).reshape(*lead, DROWS, D)


def swap(v, bit):
    n = lax.axis_size("fsdp")
    return lax.ppermute(v, "fsdp", [(i, i ^ bit) for i in range(n)])


def swap_dp(v):
    return lax.ppermute(v, "dp", [(0, 1), (1, 0)])


def add(a, b):
    return (a.astype(F32) + b.astype(F32)).astype(BF16)


def together(*values):
    return lax.optimization_barrier(values)


def z_stage(shard):
    return jnp.concatenate([shard] + [swap(shard, 4 * k) for k in (1, 2, 3)], axis=0)


def axis_stage(pieces, cut):
    left, right = pieces[:, :, :cut], pieces[:, :, cut:]
    return (
        jnp.concatenate([left, swap(left, 2)], axis=0),
        jnp.concatenate([right, swap_dp(right)], axis=0),
    )


def cross_stage(left, right):
    return swap_dp(left), swap(right, 2)


def core_stage(left, right, left2, right2):
    left, right = [left, left2], [right, right2]
    return [*left, *(swap(a, 1) for a in left), *right, *(swap(a, 1) for a in right)]


def halves(keep, got):
    m = keep.shape[0] // 2
    return add(keep[:m], got[:m]), add(keep[m:], got[m:])


def dp_halves(dp, keep, got):
    m = keep.shape[2] // 2
    def side(i):
        return add(lax.dynamic_slice_in_dim(keep, i * m, m, 2), lax.dynamic_slice_in_dim(got, i * m, m, 2))
    return side(dp), side(1 - dp)


def stage(keep, move, send):
    return halves(keep, move(send))


def over_x(keep, send):
    return stage(keep, lambda a: swap(a, 2), send)


def over_z1(keep, send):
    return stage(keep, lambda a: swap(a, 4), send)


def over_z2(keep, send):
    return add(keep, swap(send, 8))[0]


def both(part):
    part = lax.reduce_precision(part.astype(F32), 8, 7)
    return part + swap_dp(part.astype(BF16)).astype(F32)


def vector_step(v, move):
    high = lax.reduce_precision(v, 8, 7)
    low = lax.reduce_precision(v - high, 8, 7)
    got = move(jnp.concatenate([high, low], axis=0).astype(BF16)).astype(F32)
    return (high + low) + (got[: v.shape[0]] + got[v.shape[0] :])


def on_device(
    tokens, cotangent, key_valid, block_mask, row_owner, w_wide, w_down, gains, shifts,
    m_wide, v_wide, m_down, v_down, m_gain, v_gain, m_shift, v_shift,
):
    n = lax.axis_size("fsdp")
    direct = n == KB
    masks = mask_arrays(key_valid[0], block_mask[0])
    channel = jnp.arange(TILE, dtype=jnp.int32) % 3
    chan = (channel[None, :] == jnp.arange(8, dtype=jnp.int32)[:, None]).astype(BF16)
    embed = jnp.where(
        channel[:, None] == 0,
        shifts[2 * LAYERS],
        jnp.where(channel[:, None] == 1, shifts[2 * LAYERS + 1], shifts[2 * LAYERS + 2]),
    )
    x0 = tokens.astype(F32) + embed

    def places(order):
        return jnp.stack([order * WROWS, order * DROWS])

    def stored_places(order):
        return jnp.pad(places(order), ((3, 0), (0, KB)))

    ff_parts = {
        "wo": [(0, 1, 3, 32, 0, D, 0)],
        "up": [(0, 1, 3, 32, D, FF, 0)],
        "down": [(0, 1, 4, 32, D + FF, D, 0)],
    }
    if direct:
        me = lax.axis_index("fsdp")
        dp = lax.axis_index("dp")
        order = [row_owner[l] for l in range(LAYERS)]

        def owner_of(level, who):
            return jnp.sum(jnp.where(who[:, None] == jnp.arange(n, dtype=jnp.int32)[None, :], order[level][None, :], 0), axis=1)

        def near_places(level, names, size):
            axes = jnp.meshgrid(*(jnp.arange(4 if k == "z" else 2, dtype=jnp.int32) for k in names), indexing="ij")
            at = {k: a.reshape(-1) for k, a in zip(names, axes)}
            own = owner_of(level, me ^ (at["c"] + 2 * at["x"] + 4 * at["z"]))
            return own * size + (dp ^ at["d"]) * 16

        all_places = [
            jnp.concatenate(
                [
                    jnp.stack(
                        [near_places(l, "cdxz", WROWS), near_places(l, "cxdz", WROWS), near_places(l, "cxdz", DROWS)]
                    ),
                    jnp.pad(places(order[l]), ((0, 0), (0, KB))),
                ]
            )
            for l in range(LAYERS)
        ]
        half = 3 * D // 2
        att_parts = [
            {"qkv": [(0, 4, 0, 16, 0, half, 0), (4, 4, 1, 16, 0, half, half)]},
            {"qkv": [(0, 4, 0, 16, 0, 3 * D, 0)]},
        ]
        all_parts = [
            att_parts[0] | {"wo": [(8, 1, 3, 32, 0, D, 0)]},
            att_parts[1] | {"wo": [(0, 4, 0, 16, 3 * D, D, 0)]},
        ]
        ff_parts1 = {
            "wo": [(0, 4, 0, 16, 3 * D, D, 0)],
            "up": [(8, 1, 3, 32, 0, FF, 0)],
            "down": [(4, 4, 2, 16, 0, D, 0)],
        }
        low = [w_wide[l][:, 3 * D :].astype(BF16) for l in range(LAYERS)]
        low_down = [pack_down(w_down[l].astype(BF16)) for l in range(LAYERS)]
        far = [
            lax.all_gather(a, "fsdp", axis=0)
            for a in (jnp.concatenate([low[0], low_down[0]], axis=1), low[1][:, D:])
        ]
        mine = [
            lax.dynamic_slice_in_dim(a, dp * 16, 16, 0)[None]
            for a in (
                w_wide[0][:, : 3 * D].astype(BF16),
                jnp.concatenate([w_wide[1][:, : 4 * D].astype(BF16), low_down[1]], axis=1),
            )
        ]
        turn = jnp.arange(KB, dtype=jnp.int32)
        relative = me ^ (turn // 8 + 2 * ((turn // 4) % 2) + 4 * ((turn // 2) % 2) + 8 * (turn % 2))
        stored1 = places(order[1])
        relative0, relative1 = (places(owner_of(l, relative)) for l in range(LAYERS))
    else:
        att_weights = []
        natural = places(jnp.arange(KB, dtype=jnp.int32))
        all_parts = {k: [(0, 1, i, r, c + 3 * D, w, 0) for _, _, i, r, c, w, _ in v] for k, v in ff_parts.items()}
        all_parts["qkv"] = [(0, 1, 3, 32, 0, 3 * D, 0)]
        for l in range(LAYERS):
            wide = lax.all_gather(w_wide[l].astype(BF16), "fsdp", axis=0, tiled=True)
            down = lax.all_gather(w_down[l].astype(BF16), "fsdp", axis=0, tiled=True)
            wide = dn(pick_rows(row_owner[l], D // n), wide).astype(BF16).reshape(KB, WROWS, 4 * D + FF)
            down = dn(pick_rows(row_owner[l], FF // n), down).astype(BF16).reshape(KB, DROWS, D)
            full = jnp.concatenate([wide, pack_down(down)], axis=2)
            att_weights.append((stored_places(jnp.arange(KB, dtype=jnp.int32)), all_parts, [full]))
        ff_weights = att_weights

    def sum_stored(level, full):
        pick = pick_rows(row_owner[level], full.shape[0] // n)
        part = lax.psum_scatter(tn(pick, full).astype(BF16), "fsdp", scatter_dimension=0, tiled=True)
        return both(part)

    def sum_ff(level, grad):
        full = jnp.concatenate(grad, axis=0)
        up = sum_stored(level, full[..., :FF].reshape(D, FF))
        return up, sum_stored(level, unpack_down(full[..., FF:]).reshape(FF, D))

    vecs = [
        jnp.stack([gains[2 * l], shifts[2 * l], gains[2 * l + 1], shifts[2 * l + 1]])
        for l in range(LAYERS)
    ]
    def forward_of(level, att, weights):
        *kept, x = att
        r1, r2 = forward(level, x, kept[2], vecs[level], weights)
        return kept, r1, r2

    if direct:
        left, right, rest = together(*axis_stage(z_stage(mine[0]), half), mine[1])
        left, right, left2, right2, rest = together(left, right, *cross_stage(left, right), z_stage(rest))
        near0 = core_stage(left, right, left2, right2)
        state, rest, *near0 = together(x0, rest, *near0)
        sides = axis_stage(rest, 4 * D)
        *got, x = attend(0, state, vecs[0][0:2], masks, (all_places[0], att_parts[0], near0))
        got[3], *sides = together(got[3], *sides)
        cross = cross_stage(*sides)
        kept0, r1_0, r2_0 = forward_of(0, (*got, x), (all_places[0], ff_parts, far[:1]))
        r2_0, *sides = together(r2_0, *sides, *cross)
        near1 = core_stage(*sides)
        got = attend(1, r2_0, vecs[0][2:4], masks, (all_places[1], att_parts[1], near1[:4]))
        ff_weights = [(all_places[0], ff_parts, far[:1]), (all_places[1], ff_parts1, near1 + far[1:])]
        back_weights = [
            (all_places[0], all_parts[0], near0 + far[:1]),
            (all_places[1], all_parts[1], near1[:4]),
        ]
    else:
        got = attend(0, x0, vecs[0][0:2], masks, att_weights[0])
        kept0, r1_0, r2_0 = forward_of(0, got, ff_weights[0])
        got = attend(1, r2_0, vecs[0][2:4], masks, att_weights[1])
    kept1, r1_1, r2_1 = forward_of(1, got, ff_weights[1])

    ff1_places = stored1 if direct else natural
    ff1, dr1, dvec1, out_tokens = back(1, cotangent, r2_1, r1_1, vecs[1], ff_weights[1], ff1_places, 1)
    if direct:
        ff1 = lax.psum_scatter(ff1[0], "fsdp", scatter_dimension=0)
        dx, *att1 = attend_back(dr1, kept1, masks, back_weights[1], relative1)
        dx, *att1 = together(dx, *att1)
        got1 = swap(att1[1], 1)
        ff0, dr1, dvec0 = back(0, dx, r2_0, r1_0, vecs[0], ff_weights[0], relative0, 2)
        dr1, *work = together(dr1, *ff0, *halves(att1[0], got1))
        ff0, att1 = work[:2], work[2:]
        got0 = swap(ff0[1], 1)
        got1 = swap(att1[1], 2)
        dm, extra, dleft, *left = attend_left(dr1, kept0, masks, back_weights[0], relative0)
        extra, upk, ups, dok, dos, *work = together(
            extra, *halves(ff0[0][..., :FF], got0[..., :FF]), *dp_halves(dp, ff0[0][..., FF:], got0[..., FF:]),
            *left, *halves(att1[0], got1),
        )
        left, att1 = work[:2], work[2:]
        gotu = swap(ups, 2)
        gotd = swap_dp(dos)
        gotl = swap(left[1], 1)
        got1 = swap(att1[1], 4)
        dright, *right = attend_right(dm, extra, kept0, masks, relative0)
        dright, upk, ups, dok, dos, *work = together(
            dright, *dp_halves(dp, upk, gotu), *halves(dok, gotd), *halves(left[0], gotl), *right,
            *halves(att1[0], got1), ff1,
        )
        left, right, att1, ff1 = work[:2], work[2:4], work[4:6], work[6]
        gotu = swap_dp(ups)
        gotd = swap(dos, 2)
        gotl = swap(left[1], 2)
        gotr = swap(right[1], 1)
        got1 = swap(att1[1], 8)
        grad_tokens, dchan = input_grad(dr1, dleft, dright, chan, (all_places[0], att_parts[0], near0))
        att1 = add(att1[0], got1)[0]
        ff0 = [jnp.concatenate(a, axis=2) for a in zip(halves(upk, gotu), halves(dok, gotd))]
        keep0, send0, keepl, sendl, keepr, sendr, dchan, att1, ff1 = together(
            *ff0, *halves(left[0], gotl), *halves(right[0], gotr), dchan, att1, ff1
        )
        dvecs = jnp.concatenate([dvec0, dvec1], axis=0)
        vec = jnp.concatenate([dvecs[0::2], dvecs[1::2], dchan[:3]], axis=0)
        vec = vector_step(vec, lambda a: swap(a, 2))
        ff1 = both(ff1)
        keep0, send0, keepl, sendl, keepr, sendr, vec, att1, ff1 = together(
            *over_z1(keep0, send0), *over_z1(keepl, sendl), *over_x(keepr, sendr), vec, att1, ff1
        )
        att1 = both(att1)
        vec = vector_step(vec, lambda a: swap(a, 4))
        ff0, left, keepr, sendr, vec = together(
            over_z2(keep0, send0), over_z2(keepl, sendl), *over_z1(keepr, sendr), vec
        )
        vec = vector_step(vec, lambda a: swap(a, 8))
        other, left, right, vec = together(swap_dp(ff0), both(left), over_z2(keepr, sendr), vec)
        vec = vector_step(vec, swap_dp)
        right = both(right)
        vector_grad = vector_step(vec, lambda a: swap(a, 1))
        lower, upper = (jnp.where(dp == i, ff0, other).astype(F32) for i in range(2))
        ups = [jnp.concatenate([lower[:, : FF // 2], upper[:, : FF // 2]], axis=1), ff1[:, :FF]]
        down_grads = [
            unpack_down(jnp.concatenate([lower[:, FF // 2 :], upper[:, FF // 2 :]], axis=1)),
            unpack_down(ff1[:, FF:]),
        ]
        half = D // 2
        att0 = [a[:, i * half : (i + 1) * half] for i in range(3) for a in (left, right)]
        atts = [jnp.concatenate([*att0, left[:, 3 * half :]], axis=1), att1]
    else:
        dx, *att1 = attend_back(dr1, kept1, masks, att_weights[1], natural)
        ff0, dr1, dvec0 = back(0, dx, r2_0, r1_0, vecs[0], ff_weights[0], natural, 1)
        dm, extra, dleft, *left = attend_left(dr1, kept0, masks, att_weights[0], natural)
        dright, *right = attend_right(dm, extra, kept0, masks, natural)
        grad_tokens, dchan = input_grad(dr1, dleft, dright, chan, att_weights[0])
        ups, down_grads = zip(sum_ff(0, ff0), sum_ff(1, ff1))
        left, right = (jnp.concatenate(a, axis=0).reshape(D, -1) for a in (left, right))
        half = D // 2
        att0 = [a[:, i * half : (i + 1) * half] for i in range(3) for a in (left, right)]
        att0 = jnp.concatenate([*att0, left[:, 3 * half :]], axis=1)
        dvecs = jnp.concatenate([dvec0, dvec1], axis=0)
        vec = jnp.concatenate([dvecs[0::2], dvecs[1::2], dchan[:3]], axis=0)
        vector_grad = lax.psum(vec, ("fsdp", "dp"))
        atts = [sum_stored(0, att0), sum_stored(1, jnp.concatenate(att1, axis=0).reshape(D, 4 * D))]
    wide_grads = [jnp.concatenate([atts[l], ups[l]], axis=1) for l in range(LAYERS)]
    grad_gain, grad_shift = vector_grad[: 2 * LAYERS], vector_grad[2 * LAYERS :]
    grad_wide = jnp.stack(wide_grads)
    grad_down = jnp.stack(down_grads)
    new_wide, first_wide, second_wide = adamw(w_wide, grad_wide, m_wide, v_wide, MATRIX_RATE)
    new_down, first_down, second_down = adamw(w_down, grad_down, m_down, v_down, MATRIX_RATE)
    new_gains, first_gain, second_gain = adamw(gains, grad_gain, m_gain, v_gain, VECTOR_RATE)
    new_shifts, first_shift, second_shift = adamw(shifts, grad_shift, m_shift, v_shift, VECTOR_RATE)
    return (
        out_tokens,
        grad_tokens,
        new_wide,
        new_down,
        new_gains,
        new_shifts,
        first_wide,
        second_wide,
        first_down,
        second_down,
        first_gain,
        second_gain,
        first_shift,
        second_shift,
        new_wide.astype(BF16),
        new_down.astype(BF16),
    )


def solution(mesh):
    tile = P(("fsdp", "dp"))
    stored = P(None, "fsdp", None)
    in_specs = (tile, tile, tile, tile, P(), stored, stored, P(), P()) + (stored,) * 4 + (P(),) * 4
    out_specs = (tile, tile, stored, stored, P(), P()) + (stored,) * 4 + (P(),) * 4 + (stored,) * 2
    return jax.shard_map(
        on_device, mesh=mesh, in_specs=in_specs, out_specs=out_specs, check_vma=False
    )
```

```python
import functools

import jax
import jax.numpy as jnp
from jax import lax
from jax.experimental import pallas as pl
from jax.experimental.pallas import tpu as pltpu
from jax.sharding import PartitionSpec as P

D = 512
HEADS = 8
LAYERS = 2
STEP = 5
TILE = 1024
NBLK = 4
FF = 2048

NORM_EPS = 1e-05
MASKED_SCORE = -1e30
FIRST_DECAY = 0.5
SECOND_DECAY = 0.5
ADAM_EPS = 1e-08
WEIGHT_DECAY = 0.01
MATRIX_RATE = 0.02
VECTOR_RATE = 0.2

F32 = jnp.float32
BF16 = jnp.bfloat16
CH = 256
NCH = TILE // CH
KB = 16
WROWS = D // KB
DROWS = FF // KB
BLOCK_LANE = 24
SUM_LANE = 32
GELU_A = 0.7978845608028654
GELU_B = GELU_A * 0.044715
VMEM = pl.BlockSpec(memory_space=pltpu.VMEM)
SMEM = pl.BlockSpec(memory_space=pltpu.SMEM)
ANY = pl.BlockSpec(memory_space=pltpu.HBM)


def dn(a, b):
    return lax.dot_general(a, b, (((1,), (0,)), ((), ())), preferred_element_type=F32)


def nt(a, b):
    return lax.dot_general(a, b, (((1,), (1,)), ((), ())), preferred_element_type=F32)


def tn(a, b):
    return lax.dot_general(a, b, (((0,), (0,)), ((), ())), preferred_element_type=F32)


def rows(t):
    return slice(t * CH, (t + 1) * CH)


def normalize(r):
    center = jnp.mean(r, axis=-1, keepdims=True)
    centered = r - center
    variance = jnp.mean(centered * centered, axis=-1, keepdims=True)
    scale = lax.rsqrt(variance + NORM_EPS)
    return centered * scale, scale


def norm_back(dy, unit, scale, gain):
    du = dy * gain
    return scale * (
        du
        - jnp.mean(du, axis=-1, keepdims=True)
        - unit * jnp.mean(du * unit, axis=-1, keepdims=True)
    )


def load(refs, place_ref, parts, vmem, sem, down=False):
    for first, count, kind, unit, source, width, target in parts:
        j = 0
        for ref in refs[first : first + count]:
            for i in range(ref.shape[0]):
                start = pl.multiple_of(place_ref[kind, j], 16)
                j += 1
                for g in range(4 if down else 1):
                    columns = pl.ds(source + g * D, D) if down else pl.ds(source, width)
                    at = pl.ds(pl.multiple_of(start + 32 * g, 16), unit)
                    to = pl.ds(0, D) if down else pl.ds(target, width)
                    pltpu.make_async_copy(ref.at[i, :, columns], vmem.at[at, to], sem).start()


def unload(refs, place_ref, base, kind, vmem, sem):
    j = 0
    for ref in refs:
        for i in range(ref.shape[0]):
            start = pl.multiple_of(place_ref[kind, j], 16)
            j += 1
            for g in range(4 if kind else 1):
                at = pl.ds(pl.multiple_of(start + 32 * g, 16), WROWS)
                to = ref.at[i, :, pl.ds(base + g * D, D)] if kind else ref.at[i, :, pl.ds(base, vmem.shape[1])]
                pltpu.make_async_copy(vmem.at[at, :], to, sem).start()


def begin(source, target, sem):
    copy = pltpu.make_async_copy(source, target, sem)
    copy.start()
    return copy


def by_chunks(source, target, sems):
    return [begin(source.at[pl.ds(t * CH, CH), :], target.at[pl.ds(t * CH, CH), :], sems.at[t]) for t in range(NCH)]


def whole(vmem, sem):
    pltpu.make_async_copy(vmem, vmem, sem).wait()


def lane_of(shape):
    return lax.broadcasted_iota(jnp.int32, shape, len(shape) - 1)


def attend_kernel(first, parts, count, place_ref, x_hbm, vec_ref, kaug_hbm, qone_hbm, bias_hbm, *rest):
    refs = rest[:count]
    (
        xb_hbm, qkv_hbm, mixed_hbm, lse_hbm, mixed_ref, state_ref,
        x_ref, w, xb_ref, qkv_ref, lse_ref, kaug_ref, qone_ref, bias_ref, sem, sems, xsems,
    ) = rest[count:]
    states = by_chunks(x_hbm, x_ref, xsems)
    load(refs, place_ref, parts["qkv"], w, sem)
    masks = [
        begin(kaug_hbm, kaug_ref, sems.at[0]),
        begin(qone_hbm, qone_ref, sems.at[1]),
        begin(bias_hbm, bias_ref, sems.at[2]),
    ]
    for t in range(NCH):
        states[t].wait()
        x = x_ref[rows(t), :]
        if not first:
            x = normalize(x)[0] * vec_ref[0:1, :] + vec_ref[1:2, :]
        state_ref[rows(t), :] = x
        xb_ref[rows(t), :] = x.astype(BF16)
    lse_ref[...] = jnp.zeros((TILE, 128), F32)
    outs = [begin(xb_ref, xb_hbm, sems.at[3])]
    whole(w, sem)
    for t in range(NCH):
        qkv_ref[rows(t), :] = dn(xb_ref[rows(t), :], w[...]).astype(BF16)
    outs.append(begin(qkv_ref, qkv_hbm, sems.at[4]))
    for copy in masks:
        copy.wait()
    ones = jnp.ones((TILE, 128), BF16)
    lane = lane_of((CH, 128))

    def pair(hp, carry):
        at = pl.multiple_of(hp * 128, 128)
        keys = qkv_ref[:, pl.ds(D + at, 128)]
        full_keys = jnp.concatenate([keys, kaug_ref[...]], axis=1)
        full_values = jnp.concatenate([qkv_ref[:, pl.ds(2 * D + at, 128)], ones], axis=1)
        for t in range(NCH):
            queries = qkv_ref[rows(t), pl.ds(at, 128)] * jnp.asarray(0.125, BF16)
            outs = []
            for half in range(2):
                q = jnp.where((lane >= 64) == (half == 1), queries, jnp.zeros_like(queries))
                near = nt(q, keys[rows(t)]) + bias_ref[t]
                top = jnp.max(near, axis=-1, keepdims=True)
                if t:
                    far = nt(jnp.concatenate([q, qone_ref[rows(t), :]], axis=1), full_keys[: t * CH])
                    top = jnp.maximum(top, jnp.max(far, axis=-1, keepdims=True))
                    near = jnp.concatenate([far, near], axis=1)
                probs = jnp.exp(near - top).astype(BF16)
                o = dn(probs, full_values[: (t + 1) * CH])
                total = o[:, 128:]
                outs.append(o[:, :128] / total)
                here = ((lane & 7) == 2 * hp + half) & (lane < 24)
                lse_ref[rows(t), :] = jnp.where(here, top + jnp.log(total), lse_ref[rows(t), :])
            mixed_ref[rows(t), pl.ds(at, 128)] = jnp.where(lane < 64, outs[0], outs[1]).astype(BF16)
        return carry

    lax.fori_loop(0, HEADS // 2, pair, 0)
    outs.append(begin(mixed_ref, mixed_hbm, sems.at[5]))
    outs.append(begin(lse_ref, lse_hbm, sems.at[6]))
    for copy in outs:
        copy.wait()


def before_pairs(dr1_ref, mixed_ref, lse_ref, qone_ref, wo, dm, extra):
    wide = lane_of((D, 128))
    feature = lax.broadcasted_iota(jnp.int32, (D, 128), 0)
    collect = jnp.where(
        ((feature >> 6) == (wide & 7)) & (wide >= SUM_LANE) & (wide < SUM_LANE + 24), 1.0, 0.0
    ).astype(BF16)
    group = (lane_of((CH, 128)) >> 3) & 3
    for t in range(NCH):
        d = nt(dr1_ref[rows(t), :].astype(BF16), wo[...]).astype(BF16)
        dm[rows(t), :] = d
        prod = d.astype(F32) * mixed_ref[rows(t), :].astype(F32)
        high = prod.astype(BF16)
        low = (prod - high.astype(F32)).astype(BF16)
        v = lse_ref[rows(t), :] + dn(high, collect) + dn(low, collect)
        a = v.astype(BF16).astype(F32)
        b = (v - a).astype(BF16).astype(F32)
        c = v - a - b
        v = jnp.where(group == 0, a, jnp.where(group == 1, b, c))
        extra[rows(t), :] = (v + qone_ref[rows(t), :].astype(F32)).astype(BF16)


def back_pairs(start, count, qkv_ref, dm, extra, kaug_ref, bias_ref, dq, dqkv):
    one = lane_of((1, 128))
    alllane = lane_of((TILE, 128))
    width = count * 128

    def pair(i, carry):
        hp = i + start
        at = pl.multiple_of(hp * 128, 128)
        to = pl.multiple_of(i * 128, 128)
        queries = qkv_ref[:, pl.ds(at, 128)] * jnp.asarray(0.125, BF16)
        keys = qkv_ref[:, pl.ds(D + at, 128)]
        values = qkv_ref[:, pl.ds(2 * D + at, 128)]
        dmp = dm[:, pl.ds(at, 128)]
        full_q = jnp.concatenate([queries, extra[...]], axis=1)
        full_d = jnp.concatenate([dmp, extra[...]], axis=1)
        zero = jnp.zeros_like(queries)
        dks = [None] * NCH
        dvs = [None] * NCH
        for half in range(2):
            mine = (alllane >= 64) == (half == 1)
            h = 2 * hp + half
            q, k, v, g = (jnp.where(mine, a, zero) for a in (queries, keys, values, dmp))
            pick = (one & 7) == h
            sel_s = jnp.where(pick & (one < 24), -1.0, 0.0).astype(BF16)
            sel_d = jnp.where(pick & (one >= SUM_LANE) & (one < SUM_LANE + 24), -1.0, 0.0).astype(BF16)
            k8 = k * jnp.asarray(0.125, BF16)
            for c in range(NCH):
                near_k = jnp.concatenate([k[rows(c)], jnp.broadcast_to(sel_s, (CH, 128))], axis=1)
                s = nt(near_k, full_q[rows(c)]) + bias_ref[c]
                if c < NCH - 1:
                    far_k = jnp.concatenate([k[rows(c)], kaug_ref[rows(c), :] + sel_s], axis=1)
                    s = jnp.concatenate([s, nt(far_k, full_q[(c + 1) * CH :])], axis=1)
                p = jnp.exp(s)
                vf = jnp.concatenate([v[rows(c)], jnp.broadcast_to(sel_d, (CH, 128))], axis=1)
                ds = (p * nt(vf, full_d[c * CH :])).astype(BF16)
                dv = dn(p.astype(BF16), g[c * CH :])
                dk = dn(ds, q[c * CH :])
                dvs[c] = dv if half == 0 else dvs[c] + dv
                dks[c] = dk if half == 0 else dks[c] + dk
                part = tn(ds, k8[rows(c)])
                if half == 0 and c == 0:
                    dq[...] = part
                else:
                    dq[c * CH :, :] += part
        dqkv[:, pl.ds(to, 128)] = dq[...].astype(BF16)
        for c in range(NCH):
            dqkv[rows(c), pl.ds(width + to, 128)] = dks[c].astype(BF16)
            dqkv[rows(c), pl.ds(2 * width + to, 128)] = dvs[c].astype(BF16)
        return carry

    lax.fori_loop(0, count, pair, 0)


def take(hbm, vmem, sems, at, pairs=None):
    if pairs is None:
        return [begin(hbm, vmem, sems.at[at])]
    start, size = pairs
    copies = []
    for i in range(3):
        columns = pl.ds(i * D + start * 128, size * 128)
        copies.append(begin(hbm.at[:, columns], vmem.at[:, columns], sems.at[at + i]))
    return copies


def done(copies):
    for copy in copies:
        copy.wait()


def attend_back_kernel(parts, count, pairs, place_ref, gplace_ref, dr1_ref, *rest):
    mixed_hbm, qkv_hbm, lse_hbm, xb_hbm, kaug_hbm, qone_hbm, bias_hbm = rest[:7]
    refs, rest = rest[7 : 7 + count], rest[7 + count :]
    every = pairs == HEADS // 2
    if every:
        dx_hbm, keep_hbm, send_hbm, dm, extra, dqkv, dx_ref, dxsems, w, sem, *rest = rest
    else:
        dm, extra, dqkv_hbm, keep_hbm, send_hbm, dqkv, dsem, *rest = rest
    wo, dq, gw, mixed_ref, qkv_ref, lse_ref, xb_ref, kaug_ref, qone_ref, bias_ref, osem, gsem, sems = rest
    early = take(mixed_hbm, mixed_ref, sems, 0)
    load(refs, place_ref, parts["wo"], wo, osem)
    middle = take(lse_hbm, lse_ref, sems, 1) + take(qone_hbm, qone_ref, sems, 2)
    late = (
        take(qkv_hbm, qkv_ref, sems, 3, (0, pairs))
        + take(kaug_hbm, kaug_ref, sems, 6)
        + take(bias_hbm, bias_ref, sems, 7)
    )
    last = take(xb_hbm, xb_ref, sems, 8)
    if every:
        load(refs, place_ref, parts["qkv"], w, sem)
    width = 3 * pairs * 128
    done(early)
    gw[:, width:] = tn(mixed_ref[...], dr1_ref[...].astype(BF16)).astype(BF16)
    whole(wo, osem)
    done(middle)
    before_pairs(dr1_ref, mixed_ref, lse_ref, qone_ref, wo, dm, extra)
    done(late)
    back_pairs(0, pairs, qkv_ref, dm, extra, kaug_ref, bias_ref, dq, dqkv)
    outs = [] if every else [begin(dqkv, dqkv_hbm, dsem)]
    done(last)
    gw[:, :width] = tn(xb_ref[...], dqkv[...]).astype(BF16)
    unload([keep_hbm, send_hbm], gplace_ref, 0, 0, gw, gsem)
    if every:
        whole(w, sem)
        for t in range(NCH):
            dx_ref[rows(t), :] = dr1_ref[rows(t), :] + nt(dqkv[rows(t), :], w[...])
            part = pl.ds(t * CH, CH)
            outs.append(begin(dx_ref.at[part, :], dx_hbm.at[part, :], dxsems.at[t]))
    whole(gw, gsem)
    done(outs)


def right_kernel(
    gplace_ref, dm, extra, qkv_hbm, xb_hbm, kaug_hbm, bias_hbm, dqkv_hbm, keep_hbm, send_hbm,
    dqkv, dq, gw, qkv_ref, xb_ref, kaug_ref, bias_ref, gsem, sems,
):
    pairs = HEADS // 4
    early = (
        take(qkv_hbm, qkv_ref, sems, 0, (pairs, pairs))
        + take(kaug_hbm, kaug_ref, sems, 3)
        + take(bias_hbm, bias_ref, sems, 4)
    )
    late = take(xb_hbm, xb_ref, sems, 5)
    done(early)
    back_pairs(pairs, pairs, qkv_ref, dm, extra, kaug_ref, bias_ref, dq, dqkv)
    out = begin(dqkv, dqkv_hbm, sems.at[6])
    done(late)
    gw[...] = tn(xb_ref[...], dqkv[...]).astype(BF16)
    unload([keep_hbm, send_hbm], gplace_ref, 0, 0, gw, gsem)
    whole(gw, gsem)
    out.wait()


def input_kernel(parts, count, place_ref, dr1_ref, left_hbm, right_hbm, chan_ref, *rest):
    refs = rest[:count]
    dx_hbm, dchan_ref, w, left_ref, right_ref, dx_ref, sem, sems, dxsems = rest[count:]
    load(refs, place_ref, parts["qkv"], w, sem)
    loads = [begin(left_hbm, left_ref, sems.at[0]), begin(right_hbm, right_ref, sems.at[1])]
    whole(w, sem)
    done(loads)
    outs = []
    half = D // 2
    for t in range(NCH):
        grads = [
            ref[rows(t), i * half : (i + 1) * half] for i in range(3) for ref in (left_ref, right_ref)
        ]
        dx = dr1_ref[rows(t), :] + nt(jnp.concatenate(grads, axis=1), w[...])
        dx_ref[rows(t), :] = dx.astype(BF16)
        part = pl.ds(t * CH, CH)
        outs.append(begin(dx_ref.at[part, :], dx_hbm.at[part, :], dxsems.at[t]))
        pick = chan_ref[:, rows(t)]
        a = dx.astype(BF16)
        b = (dx - a.astype(F32)).astype(BF16)
        c = (dx - a.astype(F32) - b.astype(F32)).astype(BF16)
        total = dn(pick, a) + dn(pick, b) + dn(pick, c)
        dchan_ref[...] = total if t == 0 else dchan_ref[...] + total
    done(outs)


def forward_kernel(last, parts, count, place_ref, x_ref, mixed_ref, vec_ref, *rest):
    refs = rest[:count]
    if last:
        r1_ref, r2_ref, wo, w, wd, osem, sem, dsem = rest[count:]
    else:
        r1_hbm, r2_hbm, wo, w, wd, r1_ref, r2_ref, osem, sem, dsem, sems = rest[count:]
    load(refs, place_ref, parts["wo"], wo, osem)
    load(refs, place_ref, parts["up"], w, sem)
    load(refs, place_ref, parts["down"], wd, dsem, True)
    whole(wo, osem)
    for t in range(NCH):
        r1 = x_ref[rows(t), :] + dn(mixed_ref[rows(t), :], wo[...])
        r1_ref[rows(t), :] = r1
        r2_ref[rows(t), :] = normalize(r1)[0] * vec_ref[0:1, :] + vec_ref[1:2, :]
    outs = [] if last else [begin(r1_ref, r1_hbm, sems.at[NCH])]
    whole(w, sem)
    whole(wd, dsem)
    for t in range(NCH):
        back = r2_ref[rows(t), :]
        hb = back.astype(BF16)
        for c in range(FF // D):
            x = dn(hb, w[:, c * D : (c + 1) * D])
            half = 0.5 * x
            act = half + half * jnp.tanh(x * (GELU_A + GELU_B * (x * x)))
            back = back + dn(act.astype(BF16), wd[c * D : (c + 1) * D, :])
        r2_ref[rows(t), :] = back
        if not last:
            part = pl.ds(t * CH, CH)
            outs.append(begin(r2_ref.at[part, :], r2_hbm.at[part, :], sems.at[t]))
    for copy in outs:
        copy.wait()


def back_kernel(
    last, parts, count, gcount, place_ref, gplace_ref, dy_ref, r2_ref, r1_ref, vec_ref, *rest,
):
    refs = rest[:count]
    g_hbm = rest[count : count + gcount]
    dr1_ref, dvec_ref, *rest = rest[count + gcount :]
    if last:
        out_ref, w, wd, dr2, db, hb, act, dpre, gw, gd, sem, dsem, gsem, gdsem = rest
    else:
        w, wd, dr2, db, hb, act, dpre, gw, gd, sem, dsem, gsem, gdsem, r2_v, r1_v, dy_v, sems = rest
        loads = [begin(r2_ref, r2_v, sems.at[0]), begin(dy_ref, dy_v, sems.at[1]), begin(r1_ref, r1_v, sems.at[2])]
        r2_ref, r1_ref, dy_ref = r2_v, r1_v, dy_v
    load(refs, place_ref, parts["up"], w, sem)
    load(refs, place_ref, parts["down"], wd, dsem, True)
    dgain = jnp.zeros((1, D), F32)
    dshift = jnp.zeros((1, D), F32)
    if not last:
        done(loads[:2])
    for t in range(NCH):
        unit, scale = normalize(r2_ref[rows(t), :])
        dy = dy_ref[rows(t), :].astype(F32)
        if last:
            out_ref[rows(t), :] = (unit * vec_ref[2:3, :] + vec_ref[3:4, :]).astype(BF16)
        dgain += jnp.sum(dy * unit, axis=0, keepdims=True)
        dshift += jnp.sum(dy, axis=0, keepdims=True)
        dr = norm_back(dy, unit, scale, vec_ref[2:3, :])
        dr2[rows(t), :] = dr
        db[rows(t), :] = dr.astype(BF16)
    if not last:
        loads[2].wait()
    for t in range(NCH):
        h = normalize(r1_ref[rows(t), :])[0] * vec_ref[0:1, :] + vec_ref[1:2, :]
        hb[rows(t), :] = h.astype(BF16)
    dvec_ref[2:3, :] = dgain
    dvec_ref[3:4, :] = dshift
    whole(w, sem)
    whole(wd, dsem)
    for t in range(NCH):
        for c in range(FF // D):
            cols = slice(c * D, (c + 1) * D)
            x = dn(hb[rows(t), :], w[:, cols])
            dact = nt(db[rows(t), :], wd[cols, :])
            half = 0.5 * x
            x2 = x * x
            th = jnp.tanh(x * (GELU_A + GELU_B * x2))
            act[rows(t), cols] = (half + half * th).astype(BF16)
            slope = (0.5 + 0.5 * th) + (half - half * (th * th)) * (GELU_A + 3 * GELU_B * x2)
            dp = (dact * slope).astype(BF16)
            dpre[rows(t), cols] = dp
            dr2[rows(t), :] += nt(dp, w[:, cols])
    for c in range(FF // D):
        cols = slice(c * D, (c + 1) * D)
        gd[cols, :] = tn(act[:, cols], db[...]).astype(BF16)
    unload(g_hbm if last else g_hbm[2:], gplace_ref, FF if last else 0, 1, gd, gdsem)
    for c in range(FF // D):
        cols = slice(c * D, (c + 1) * D)
        gw[:, cols] = tn(hb[...], dpre[:, cols]).astype(BF16)
    unload(g_hbm if last else g_hbm[:2], gplace_ref, 0, 0, gw, gsem)
    dgain = jnp.zeros((1, D), F32)
    dshift = jnp.zeros((1, D), F32)
    for t in range(NCH):
        unit, scale = normalize(r1_ref[rows(t), :])
        dy = dr2[rows(t), :]
        dgain += jnp.sum(dy * unit, axis=0, keepdims=True)
        dshift += jnp.sum(dy, axis=0, keepdims=True)
        dr1_ref[rows(t), :] = norm_back(dy, unit, scale, vec_ref[0:1, :])
    dvec_ref[0:1, :] = dgain
    dvec_ref[1:2, :] = dshift
    whole(gd, gdsem)
    whole(gw, gsem)


def sds(shape, dtype=F32):
    return jax.ShapeDtypeStruct(shape, dtype)


KEPT = "kept"


def call(kernel, name, us, mib, outs, in_specs, out_specs, scratch, aliases=None):
    spaces = {id(KEPT): pltpu.VMEM, id(ANY): pltpu.HBM}

    def kept(shape, spec):
        space = spaces.get(id(spec))
        return space(shape.shape, shape.dtype) if space else shape

    def run(*args):
        args = [
            pltpu.with_memory_space_constraint(a, spaces[id(s)]) if id(s) in spaces else a
            for a, s in zip(args, in_specs)
        ]
        return pl.pallas_call(
            kernel,
            out_shape=[kept(o, s) for o, s in zip(outs, out_specs)],
            in_specs=[VMEM if s is KEPT else s for s in in_specs],
            out_specs=[VMEM if s is KEPT else s for s in out_specs],
            scratch_shapes=scratch,
            input_output_aliases=aliases or {},
            compiler_params=pltpu.CompilerParams(vmem_limit_bytes=mib * 1024 * 1024),
            cost_estimate=pl.CostEstimate(flops=us * 400000000, transcendentals=0, bytes_accessed=us * 1200000),
            name=name,
        )(*args)

    return run


DMA = pltpu.SemaphoreType.DMA


def mask_scratch():
    return [pltpu.VMEM((TILE, 128), BF16), pltpu.VMEM((TILE, 128), BF16), pltpu.VMEM((NCH, CH, CH), F32)]


def attend(level, x, vec, masks, weights):
    kaug, qone, bias, _ = masks
    place, parts, bufs = weights
    return call(
        functools.partial(attend_kernel, level == 0, parts, len(bufs)),
        f"attend{level}",
        18,
        28,
        [sds((TILE, D), BF16), sds((TILE, 3 * D), BF16), sds((TILE, D), BF16), sds((TILE, 128))]
        + [sds((TILE, D), BF16), sds((TILE, D))],
        [SMEM, ANY, VMEM] + [ANY] * (3 + len(bufs)),
        [ANY] * 4 + [KEPT] * 2,
        [
            pltpu.VMEM((TILE, D), F32),
            pltpu.VMEM((D, 3 * D), BF16),
            pltpu.VMEM((TILE, D), BF16),
            pltpu.VMEM((TILE, 3 * D), BF16),
            pltpu.VMEM((TILE, 128), F32),
            *mask_scratch(),
            DMA,
            pltpu.SemaphoreType.DMA((7,)),
            pltpu.SemaphoreType.DMA((NCH,)),
        ],
    )(place, x, vec, kaug, qone, bias, *bufs)


def grad_pair(columns):
    return [sds((KB // 2, WROWS, columns), BF16)] * 2


def attend_back(dr1, kept, masks, weights, gplace, pairs=HEADS // 2):
    kaug, qone, _, bias = masks
    place, parts, bufs = weights
    xb, qkv, mixed, lse = kept
    every = pairs == HEADS // 2
    width = 3 * pairs * 128
    pieces = grad_pair(width + D)
    own = [sds((TILE, D), BF16), sds((TILE, 128), BF16), sds((TILE, width), BF16)]
    if every:
        scratch = [pltpu.VMEM(o.shape, o.dtype) for o in own]
        scratch += [pltpu.VMEM((TILE, D), F32), pltpu.SemaphoreType.DMA((NCH,)), pltpu.VMEM((D, 3 * D), BF16), DMA]
    else:
        scratch = [pltpu.VMEM((TILE, width), BF16), DMA]
    return call(
        functools.partial(attend_back_kernel, parts, len(bufs), pairs),
        "attend_back" if every else "attend_left",
        28 if every else 17,
        34 if every else 28,
        [sds((TILE, D))] + pieces if every else own + pieces,
        [SMEM] * 2 + [KEPT] + [ANY] * (7 + len(bufs)),
        ([ANY] if every else [KEPT, KEPT, ANY]) + [ANY] * 2,
        scratch
        + [
            pltpu.VMEM((D, D), BF16),
            pltpu.VMEM((TILE, 128), F32),
            pltpu.VMEM((D, width + D), BF16),
            pltpu.VMEM((TILE, D), BF16),
            pltpu.VMEM((TILE, 3 * D), BF16),
            pltpu.VMEM((TILE, 128), F32),
            pltpu.VMEM((TILE, D), BF16),
            *mask_scratch(),
            DMA,
            DMA,
            pltpu.SemaphoreType.DMA((9,)),
        ],
    )(place, gplace, dr1, mixed, qkv, lse, xb, kaug, qone, bias, *bufs)


def attend_left(dr1, kept, masks, weights, gplace):
    return attend_back(dr1, kept, masks, weights, gplace, HEADS // 4)


def attend_right(dm, extra, kept, masks, gplace):
    kaug, _, _, bias = masks
    xb, qkv = kept[:2]
    scratch = mask_scratch()
    return call(
        right_kernel,
        "attend_right",
        14,
        24,
        [sds((TILE, 3 * D // 2), BF16)] + grad_pair(3 * D // 2),
        [SMEM, KEPT, KEPT] + [ANY] * 4,
        [ANY, ANY, ANY],
        [
            pltpu.VMEM((TILE, 3 * D // 2), BF16),
            pltpu.VMEM((TILE, 128), F32),
            pltpu.VMEM((D, 3 * D // 2), BF16),
            pltpu.VMEM((TILE, 3 * D), BF16),
            pltpu.VMEM((TILE, D), BF16),
            scratch[0],
            scratch[2],
            DMA,
            pltpu.SemaphoreType.DMA((7,)),
        ],
    )(gplace, dm, extra, qkv, xb, kaug, bias)


def input_grad(dr1, left, right, chan, weights):
    place, parts, bufs = weights
    return call(
        functools.partial(input_kernel, parts, len(bufs)),
        "input_grad",
        30,
        20,
        [sds((TILE, D), BF16), sds((8, D))],
        [SMEM, KEPT, ANY, ANY, VMEM] + [ANY] * len(bufs),
        [ANY, VMEM],
        [
            pltpu.VMEM((D, 3 * D), BF16),
            pltpu.VMEM((TILE, 3 * D // 2), BF16),
            pltpu.VMEM((TILE, 3 * D // 2), BF16),
            pltpu.VMEM((TILE, D), BF16),
            DMA,
            pltpu.SemaphoreType.DMA((2,)),
            pltpu.SemaphoreType.DMA((NCH,)),
        ],
    )(place, dr1, left, right, chan, *bufs)


def forward(level, x, mixed, vec, weights):
    place, parts, bufs = weights
    last = level == LAYERS - 1
    state = sds((TILE, D))
    return call(
        functools.partial(forward_kernel, last, parts, len(bufs)),
        f"forward{level}",
        13,
        26,
        [state] * 2,
        [SMEM, KEPT, KEPT, VMEM] + [ANY] * len(bufs),
        [KEPT] * 2 if last else [ANY] * 2,
        [pltpu.VMEM((D, D), BF16), pltpu.VMEM((D, FF), BF16), pltpu.VMEM((FF, D), BF16)]
        + ([] if last else [pltpu.VMEM((TILE, D), F32)] * 2)
        + [DMA] * 3
        + ([] if last else [pltpu.SemaphoreType.DMA((NCH + 1,))]),
    )(place, x, mixed, vec, *bufs)


def back(level, dy, r2, r1, vec, weights, gplace):
    place, parts, bufs = weights
    last = level == LAYERS - 1
    grads = [sds((KB, WROWS, 2 * FF), BF16)] if last else grad_pair(FF) * 2
    split = len(grads)
    outs = grads + [sds((TILE, D)), sds((4, D))]
    specs = [ANY] * split + [KEPT, VMEM]
    if last:
        outs.append(sds((TILE, D), BF16))
        specs.append(VMEM)
    got = call(
        functools.partial(back_kernel, last, parts, len(bufs), split),
        f"back{level}",
        24,
        42,
        outs,
        [SMEM] * 2 + [VMEM if last else ANY] + [KEPT if last else ANY] * 2 + [VMEM] + [ANY] * len(bufs),
        specs,
        [
            pltpu.VMEM((D, FF), BF16),
            pltpu.VMEM((FF, D), BF16),
            pltpu.VMEM((TILE, D), F32),
            pltpu.VMEM((TILE, D), BF16),
            pltpu.VMEM((TILE, D), BF16),
            pltpu.VMEM((TILE, FF), BF16),
            pltpu.VMEM((TILE, FF), BF16),
            pltpu.VMEM((D, FF), BF16),
            pltpu.VMEM((FF, D), BF16),
            DMA,
            DMA,
            DMA,
            DMA,
        ]
        + ([] if last else [pltpu.VMEM((TILE, D), F32)] * 3 + [pltpu.SemaphoreType.DMA((3,))]),
    )(place, gplace, dy, r2, r1, vec, *bufs)
    return got[:split], *got[split:]


def adamw(weight, grad, first, second, rate):
    first_new = FIRST_DECAY * first + (1.0 - FIRST_DECAY) * grad
    second_new = SECOND_DECAY * second + (1.0 - SECOND_DECAY) * grad * grad
    first_fix = 1.0 - FIRST_DECAY**STEP
    second_fix = 1.0 - SECOND_DECAY**STEP
    update = (
        first_new / first_fix / (jnp.sqrt(second_new / second_fix) + ADAM_EPS)
        + WEIGHT_DECAY * weight
    )
    return (weight - rate * update, first_new, second_new)


def update_kernel(dp_ref, main_ref, other_ref, right_ref, got_ref, *rest):
    states, rest = rest[:6], rest[14:]
    outs, (wide, down, loads, stores) = rest[:8], (rest[8:12], rest[12:16], rest[16], rest[17])
    copies = [
        begin(a.at[0], b, loads.at[i]) for i, (a, b) in enumerate(zip(states, (*wide[:3], *down[:3])))
    ]
    half = D // 2

    def step(held, place, grad):
        w, m, v, low = held
        new, first, second = adamw(w[place], grad, m[place], v[place], MATRIX_RATE)
        w[place], m[place], v[place], low[place] = new, first, second, new.astype(BF16)

    def columns(start, size):
        return slice(0, WROWS), slice(start, start + size)

    done(copies)
    for i in range(2):
        part = jnp.where(dp_ref[0] == i, main_ref[:, :FF].astype(F32), other_ref[:, :FF].astype(F32))
        step(wide, columns(4 * D + i * FF // 2, FF // 2), part[:, : FF // 2])
        for g in range(2):
            at = (2 * i + g) * WROWS
            step(down, (slice(at, at + WROWS), slice(0, D)), part[:, FF // 2 + g * D : FF // 2 + (g + 1) * D])
    lefts = [(FF + i * half, i * D, half) for i in range(3)] + [(FF + 3 * half, 3 * D, D)]
    rights = [(i * half, i * D + half, half) for i in range(3)]
    for pieces, mine, theirs in ((lefts, main_ref, other_ref), (rights, right_ref, got_ref)):
        for source, target, size in pieces:
            at = slice(source, source + size)
            step(wide, columns(target, size), mine[:, at].astype(F32) + theirs[:, at].astype(F32))
    done([begin(b, a.at[0], stores.at[i]) for i, (a, b) in enumerate(zip(outs, (*wide, *down)))])


def update_first(dp, main, other, right, got, states, results):
    def held(rows_, columns):
        return [pltpu.VMEM((rows_, columns), F32)] * 3 + [pltpu.VMEM((rows_, columns), BF16)]

    return call(
        update_kernel,
        "update",
        3,
        12,
        [sds(r.shape, r.dtype) for r in results],
        [SMEM] + [VMEM] * 4 + [ANY] * 14,
        [ANY] * 8,
        held(WROWS, 4 * D + FF) + held(DROWS, D) + [pltpu.SemaphoreType.DMA((6,)), pltpu.SemaphoreType.DMA((8,))],
        {11 + i: i for i in range(8)},
    )(dp.reshape(1), main, other, right, got, *states, *results)


def mask_arrays(valid_count, table):
    places = jnp.arange(TILE, dtype=jnp.int32)
    block = (places >> 9) * 2 + ((places >> 5) & 1)
    member = block[:, None] == jnp.arange(NBLK, dtype=jnp.int32)[None, :]
    open_to = jnp.any(member[:, None, :] & (table[None] == 1), axis=-1) & (places < valid_count)[:, None]
    penalty = jnp.where(open_to, 0.0, MASKED_SCORE).astype(F32)
    pads = ((0, 0), (BLOCK_LANE, 128 - BLOCK_LANE - NBLK))
    kaug = jnp.pad(penalty, pads).astype(BF16)
    qone = jnp.pad(member.astype(F32), pads).astype(BF16)
    near = jnp.arange(CH, dtype=jnp.int32)
    visible = jnp.any(
        member.reshape(NCH, CH, 1, NBLK) & open_to.reshape(NCH, 1, CH, NBLK), axis=-1
    ) & (near[None, :] <= near[:, None])
    visible = visible | (near[None, :] == near[:, None])
    bias = jnp.where(visible, 0.0, MASKED_SCORE).astype(F32)
    return kaug, qone, bias, bias.transpose(0, 2, 1)


def pick_rows(order, size):
    n = order.shape[0]
    place = (order[:, None] * size + jnp.arange(size, dtype=jnp.int32)[None, :]).reshape(-1)
    return (place[None, :] == jnp.arange(n * size, dtype=jnp.int32)[:, None]).astype(BF16)


def pack_down(down):
    lead = down.shape[:-2]
    return jnp.swapaxes(down.reshape(*lead, 4, WROWS, D), -3, -2).reshape(*lead, WROWS, FF)


def unpack_down(packed):
    lead = packed.shape[:-2]
    return jnp.swapaxes(packed.reshape(*lead, WROWS, 4, D), -3, -2).reshape(*lead, DROWS, D)


def swap(v, bit):
    n = lax.axis_size("fsdp")
    return lax.ppermute(v, "fsdp", [(i, i ^ bit) for i in range(n)])


def swap_dp(v):
    return lax.ppermute(v, "dp", [(0, 1), (1, 0)])


def add(a, b):
    return (a.astype(F32) + b.astype(F32)).astype(BF16)


def together(*values):
    return lax.optimization_barrier(values)


def z_stage(shard):
    return jnp.concatenate([shard] + [swap(shard, 4 * k) for k in (1, 2, 3)], axis=0)


def axis_stage(pieces, cut):
    left, right = pieces[:, :, :cut], pieces[:, :, cut:]
    return (
        jnp.concatenate([left, swap(left, 2)], axis=0),
        jnp.concatenate([right, swap_dp(right)], axis=0),
    )


def cross_stage(left, right):
    return swap_dp(left), swap(right, 2)


def core_stage(left, right, left2, right2):
    left, right = [left, left2], [right, right2]
    return [*left, *(swap(a, 1) for a in left), *right, *(swap(a, 1) for a in right)]


def halves(keep, got):
    m = keep.shape[0] // 2
    return add(keep[:m], got[:m]), add(keep[m:], got[m:])


def dp_halves(dp, keep, got):
    m = keep.shape[2] // 2
    def side(i):
        return add(lax.dynamic_slice_in_dim(keep, i * m, m, 2), lax.dynamic_slice_in_dim(got, i * m, m, 2))
    return side(dp), side(1 - dp)


def stage(keep, move, send):
    return halves(keep, move(send))


def over_x(keep, send):
    return stage(keep, lambda a: swap(a, 2), send)


def over_z1(keep, send):
    return stage(keep, lambda a: swap(a, 4), send)


def over_z2(keep, send):
    return add(keep, swap(send, 8))[0]


def both(part):
    part = lax.reduce_precision(part.astype(F32), 8, 7)
    return part + swap_dp(part.astype(BF16)).astype(F32)


def split_halves(part):
    m = part.shape[0] // 2
    return part[:m], part[m:]


def with_vector(keep, send, v, move):
    high = lax.reduce_precision(v, 8, 7)
    low = lax.reduce_precision(v - high, 8, 7)
    block = jnp.pad(jnp.concatenate([high, low], axis=0).astype(BF16), ((0, 10), (0, send.shape[2] - D)))
    got = move(jnp.concatenate([send, block[None]], axis=0))
    part = got[0] if keep is None else add(keep, got[:-1])
    there = got[-1, :22, :D].astype(F32)
    return part, (high + low) + (there[:11] + there[11:])


def vector_step(v, move):
    high = lax.reduce_precision(v, 8, 7)
    low = lax.reduce_precision(v - high, 8, 7)
    got = move(jnp.concatenate([high, low], axis=0).astype(BF16)).astype(F32)
    return (high + low) + (got[: v.shape[0]] + got[v.shape[0] :])


def on_device(
    tokens, cotangent, key_valid, block_mask, row_owner, w_wide, w_down, gains, shifts,
    m_wide, v_wide, m_down, v_down, m_gain, v_gain, m_shift, v_shift,
):
    n = lax.axis_size("fsdp")
    direct = n == KB
    masks = mask_arrays(key_valid[0], block_mask[0])
    channel = jnp.arange(TILE, dtype=jnp.int32) % 3
    chan = (channel[None, :] == jnp.arange(8, dtype=jnp.int32)[:, None]).astype(BF16)
    embed = jnp.where(
        channel[:, None] == 0,
        shifts[2 * LAYERS],
        jnp.where(channel[:, None] == 1, shifts[2 * LAYERS + 1], shifts[2 * LAYERS + 2]),
    )
    x0 = tokens.astype(F32) + embed

    def places(order):
        return jnp.stack([order * WROWS, order * DROWS])

    def stored_places(order):
        return jnp.pad(places(order), ((3, 0), (0, KB)))

    ff_parts = {
        "wo": [(0, 1, 3, 32, 0, D, 0)],
        "up": [(0, 1, 3, 32, D, FF, 0)],
        "down": [(0, 1, 4, 32, D + FF, D, 0)],
    }
    if direct:
        me = lax.axis_index("fsdp")
        dp = lax.axis_index("dp")
        order = [row_owner[l] for l in range(LAYERS)]

        def owner_of(level, who):
            return jnp.sum(jnp.where(who[:, None] == jnp.arange(n, dtype=jnp.int32)[None, :], order[level][None, :], 0), axis=1)

        def near_places(level, names, size):
            axes = jnp.meshgrid(*(jnp.arange(4 if k == "z" else 2, dtype=jnp.int32) for k in names), indexing="ij")
            at = {k: a.reshape(-1) for k, a in zip(names, axes)}
            own = owner_of(level, me ^ (at["c"] + 2 * at["x"] + 4 * at["z"]))
            return own * size + (dp ^ at["d"]) * 16

        all_places = [
            jnp.concatenate(
                [
                    jnp.stack(
                        [near_places(l, "cdxz", WROWS), near_places(l, "cxdz", WROWS), near_places(l, "cxdz", DROWS)]
                    ),
                    jnp.pad(places(order[l]), ((0, 0), (0, KB))),
                ]
            )
            for l in range(LAYERS)
        ]
        half = 3 * D // 2
        att_parts = [
            {"qkv": [(0, 4, 0, 16, 0, half, 0), (4, 4, 1, 16, 0, half, half)]},
            {"qkv": [(0, 4, 0, 16, 0, 3 * D, 0)]},
        ]
        all_parts = [
            att_parts[0] | {"wo": [(8, 1, 3, 32, 0, D, 0)]},
            att_parts[1] | {"wo": [(0, 4, 0, 16, 3 * D, D, 0)]},
        ]
        ff_parts1 = {
            "wo": [(0, 4, 0, 16, 3 * D, D, 0)],
            "up": [(8, 1, 3, 32, 0, FF, 0)],
            "down": [(4, 4, 2, 16, 0, D, 0)],
        }
        low = [w_wide[l][:, 3 * D :].astype(BF16) for l in range(LAYERS)]
        packed_down = [pack_down(w_down[l].astype(BF16)) for l in range(LAYERS)]
        far = [
            lax.all_gather(a, "fsdp", axis=0)
            for a in (jnp.concatenate([low[0], packed_down[0]], axis=1), low[1][:, D:])
        ]
        mine = [
            lax.dynamic_slice_in_dim(a, dp * 16, 16, 0)[None]
            for a in (
                w_wide[0][:, : 3 * D].astype(BF16),
                jnp.concatenate([w_wide[1][:, : 4 * D].astype(BF16), packed_down[1]], axis=1),
            )
        ]
        turn = jnp.arange(KB, dtype=jnp.int32)
        relative = me ^ (turn // 8 + 2 * ((turn // 4) % 2) + 4 * ((turn // 2) % 2) + 8 * (turn % 2))
        stored1 = places(order[1])
        relative0, relative1 = (places(owner_of(l, relative)) for l in range(LAYERS))
    else:
        att_weights = []
        natural = places(jnp.arange(KB, dtype=jnp.int32))
        all_parts = {k: [(0, 1, i, r, c + 3 * D, w, 0) for _, _, i, r, c, w, _ in v] for k, v in ff_parts.items()}
        all_parts["qkv"] = [(0, 1, 3, 32, 0, 3 * D, 0)]
        for l in range(LAYERS):
            wide = lax.all_gather(w_wide[l].astype(BF16), "fsdp", axis=0, tiled=True)
            down = lax.all_gather(w_down[l].astype(BF16), "fsdp", axis=0, tiled=True)
            wide = dn(pick_rows(row_owner[l], D // n), wide).astype(BF16).reshape(KB, WROWS, 4 * D + FF)
            down = dn(pick_rows(row_owner[l], FF // n), down).astype(BF16).reshape(KB, DROWS, D)
            full = jnp.concatenate([wide, pack_down(down)], axis=2)
            att_weights.append((stored_places(jnp.arange(KB, dtype=jnp.int32)), all_parts, [full]))
        ff_weights = att_weights

    def sum_stored(level, full):
        pick = pick_rows(row_owner[level], full.shape[0] // n)
        part = lax.psum_scatter(tn(pick, full).astype(BF16), "fsdp", scatter_dimension=0, tiled=True)
        return both(part)

    def sum_ff(level, grad):
        if level:
            up, down = grad[0][..., :FF], grad[0][..., FF:]
        else:
            up, down = jnp.concatenate(grad[:2], axis=0), jnp.concatenate(grad[2:], axis=0)
        return sum_stored(level, up.reshape(D, FF)), sum_stored(level, unpack_down(down).reshape(FF, D))

    vecs = [
        jnp.stack([gains[2 * l], shifts[2 * l], gains[2 * l + 1], shifts[2 * l + 1]])
        for l in range(LAYERS)
    ]
    def forward_of(level, att, weights):
        *kept, mixed, x = att
        r1, r2 = forward(level, x, mixed, vecs[level], weights)
        return kept, r1, r2

    if direct:
        left, right, rest = together(*axis_stage(z_stage(mine[0]), half), mine[1])
        rest = z_stage(rest)
        left, right, left2, right2 = together(left, right, *cross_stage(left, right))
        near0 = core_stage(left, right, left2, right2)
        state, rest, *near0 = together(x0, rest, *near0)
        sides = axis_stage(rest, 4 * D)
        got = list(attend(0, state, vecs[0][0:2], masks, (all_places[0], att_parts[0], near0)))
        got[5], *sides = together(got[5], *sides)
        cross = cross_stage(*sides)
        kept0, r1_0, r2_0 = forward_of(0, got, (all_places[0], ff_parts, far[:1]))
        r2_0, *sides = together(r2_0, *sides, *cross)
        near1 = core_stage(*sides)
        got = attend(1, r2_0, vecs[0][2:4], masks, (all_places[1], att_parts[1], near1[:4]))
        ff_weights = [(all_places[0], ff_parts, far[:1]), (all_places[1], ff_parts1, near1 + far[1:])]
        back_weights = [
            (all_places[0], all_parts[0], near0 + far[:1]),
            (all_places[1], all_parts[1], near1[:4]),
        ]
    else:
        got = attend(0, x0, vecs[0][0:2], masks, att_weights[0])
        kept0, r1_0, r2_0 = forward_of(0, got, ff_weights[0])
        got = attend(1, r2_0, vecs[0][2:4], masks, att_weights[1])
    kept1, r1_1, r2_1 = forward_of(1, got, ff_weights[1])

    ff1_places = stored1 if direct else natural
    ff1, dr1, dvec1, out_tokens = back(1, cotangent, r2_1, r1_1, vecs[1], ff_weights[1], ff1_places)
    if direct:
        ff1 = lax.psum_scatter(ff1[0], "fsdp", scatter_dimension=0)
        dx, *att1 = attend_back(dr1, kept1, masks, back_weights[1], relative1)
        dx, *att1 = together(dx, *att1)
        got1 = swap(att1[1], 1)
        ff0, dr1, dvec0 = back(0, dx, r2_0, r1_0, vecs[0], ff_weights[0], relative0)
        dr1, *work = together(dr1, *ff0, *halves(att1[0], got1))
        ff0, att1 = work[:4], work[4:]
        gotu = swap(ff0[1], 1)
        gotd = swap(ff0[3], 1)
        got1 = swap(att1[1], 2)
        dm, extra, dleft, *left = attend_left(dr1, kept0, masks, back_weights[0], relative0)
        extra, upk, ups, dok, dos, *work = together(
            extra, *halves(ff0[0], gotu), *dp_halves(dp, ff0[2], gotd), *left, *halves(att1[0], got1),
        )
        left, att1 = work[:2], work[2:]
        gotu = swap(ups, 2)
        gotd = swap_dp(dos)
        gotl = swap(left[1], 1)
        got1 = swap(att1[1], 4)
        dright, *right = attend_right(dm, extra, kept0, masks, relative0)
        dright, upk, ups, dok, dos, *work = together(
            dright, *dp_halves(dp, upk, gotu), *halves(dok, gotd), *halves(left[0], gotl), *right,
            *halves(att1[0], got1), ff1,
        )
        left, right, att1, ff1 = work[:2], work[2:4], work[4:6], work[6]
        gotu = swap_dp(ups)
        gotd = swap(dos, 2)
        gotl = swap(left[1], 2)
        gotr = swap(right[1], 1)
        got1 = swap(att1[1], 8)
        grad_tokens, dchan = input_grad(dr1, dleft, dright, chan, (all_places[0], att_parts[0], near0))
        att1 = add(att1[0], got1)[0]
        main = [jnp.concatenate(a, axis=2) for a in zip(halves(upk, gotu), halves(dok, gotd), halves(left[0], gotl))]
        keep, send, keepr, sendr, dchan, att1, ff1 = together(*main, *halves(right[0], gotr), dchan, att1, ff1)
        dvecs = jnp.concatenate([dvec0, dvec1], axis=0)
        vec = jnp.concatenate([dvecs[0::2], dvecs[1::2], dchan[:3]], axis=0)
        right, vec = with_vector(keepr, sendr, vec, lambda a: swap(a, 2))
        ff1 = both(ff1)
        keep, send, keepr, sendr, vec, att1, ff1 = together(
            *over_z1(keep, send), *split_halves(right), vec, att1, ff1
        )
        right, vec = with_vector(keepr, sendr, vec, lambda a: swap(a, 4))
        att1 = both(att1)
        main, keepr, sendr, vec, att1 = together(over_z2(keep, send), *split_halves(right), vec, att1)
        right, vec = with_vector(keepr, sendr, vec, lambda a: swap(a, 8))
        other, right, vec = together(swap_dp(main), right[0], vec)
        got, vec = with_vector(None, right[None], vec, swap_dp)
        vector_grad = vector_step(vec, lambda a: swap(a, 1))
        ups = [jnp.zeros((WROWS, FF), F32), ff1[:, :FF]]
        down_grads = [jnp.zeros((DROWS, D), F32), unpack_down(ff1[:, FF:])]
        atts = [jnp.zeros((WROWS, 4 * D), F32), att1]
    else:
        dx, *att1 = attend_back(dr1, kept1, masks, att_weights[1], natural)
        ff0, dr1, dvec0 = back(0, dx, r2_0, r1_0, vecs[0], ff_weights[0], natural)
        dm, extra, dleft, *left = attend_left(dr1, kept0, masks, att_weights[0], natural)
        dright, *right = attend_right(dm, extra, kept0, masks, natural)
        grad_tokens, dchan = input_grad(dr1, dleft, dright, chan, att_weights[0])
        ups, down_grads = zip(sum_ff(0, ff0), sum_ff(1, ff1))
        left, right = (jnp.concatenate(a, axis=0).reshape(D, -1) for a in (left, right))
        half = D // 2
        att0 = [a[:, i * half : (i + 1) * half] for i in range(3) for a in (left, right)]
        att0 = jnp.concatenate([*att0, left[:, 3 * half :]], axis=1)
        dvecs = jnp.concatenate([dvec0, dvec1], axis=0)
        vec = jnp.concatenate([dvecs[0::2], dvecs[1::2], dchan[:3]], axis=0)
        vector_grad = lax.psum(vec, ("fsdp", "dp"))
        atts = [sum_stored(0, att0), sum_stored(1, jnp.concatenate(att1, axis=0).reshape(D, 4 * D))]
    wide_grads = [jnp.concatenate([atts[l], ups[l]], axis=1) for l in range(LAYERS)]
    grad_gain, grad_shift = vector_grad[: 2 * LAYERS], vector_grad[2 * LAYERS :]
    grad_wide = jnp.stack(wide_grads)
    grad_down = jnp.stack(down_grads)
    new_wide, first_wide, second_wide = adamw(w_wide, grad_wide, m_wide, v_wide, MATRIX_RATE)
    new_down, first_down, second_down = adamw(w_down, grad_down, m_down, v_down, MATRIX_RATE)
    low_wide, low_down = new_wide.astype(BF16), new_down.astype(BF16)
    if direct:
        (
            new_wide, first_wide, second_wide, low_wide, new_down, first_down, second_down, low_down
        ) = update_first(
            dp, main, other, right, got,
            (w_wide, m_wide, v_wide, w_down, m_down, v_down),
            (new_wide, first_wide, second_wide, low_wide, new_down, first_down, second_down, low_down),
        )
    new_gains, first_gain, second_gain = adamw(gains, grad_gain, m_gain, v_gain, VECTOR_RATE)
    new_shifts, first_shift, second_shift = adamw(shifts, grad_shift, m_shift, v_shift, VECTOR_RATE)
    return (
        out_tokens,
        grad_tokens,
        new_wide,
        new_down,
        new_gains,
        new_shifts,
        first_wide,
        second_wide,
        first_down,
        second_down,
        first_gain,
        second_gain,
        first_shift,
        second_shift,
        low_wide,
        low_down,
    )


def solution(mesh):
    tile = P(("fsdp", "dp"))
    stored = P(None, "fsdp", None)
    in_specs = (tile, tile, tile, tile, P(), stored, stored, P(), P()) + (stored,) * 4 + (P(),) * 4
    out_specs = (tile, tile, stored, stored, P(), P()) + (stored,) * 4 + (P(),) * 4 + (stored,) * 2
    return jax.shard_map(
        on_device, mesh=mesh, in_specs=in_specs, out_specs=out_specs, check_vma=False
    )
```

```python
import functools

import jax
import jax.numpy as jnp
from jax import lax
from jax.experimental import pallas as pl
from jax.experimental.pallas import tpu as pltpu
from jax.sharding import PartitionSpec as P

D = 512
HEADS = 8
LAYERS = 2
STEP = 5
TILE = 1024
NBLK = 4
FF = 2048

NORM_EPS = 1e-05
MASKED_SCORE = -1e30
FIRST_DECAY = 0.5
SECOND_DECAY = 0.5
ADAM_EPS = 1e-08
WEIGHT_DECAY = 0.01
MATRIX_RATE = 0.02
VECTOR_RATE = 0.2

F32 = jnp.float32
BF16 = jnp.bfloat16
CH = 256
NCH = TILE // CH
KB = 16
WROWS = D // KB
DROWS = FF // KB
BLOCK_LANE = 24
SUM_LANE = 32
GELU_A = 0.7978845608028654
GELU_B = GELU_A * 0.044715
VMEM = pl.BlockSpec(memory_space=pltpu.VMEM)
SMEM = pl.BlockSpec(memory_space=pltpu.SMEM)
ANY = pl.BlockSpec(memory_space=pltpu.HBM)


def dn(a, b):
    return lax.dot_general(a, b, (((1,), (0,)), ((), ())), preferred_element_type=F32)


def nt(a, b):
    return lax.dot_general(a, b, (((1,), (1,)), ((), ())), preferred_element_type=F32)


def tn(a, b):
    return lax.dot_general(a, b, (((0,), (0,)), ((), ())), preferred_element_type=F32)


def rows(t):
    return slice(t * CH, (t + 1) * CH)


def normalize(r):
    center = jnp.mean(r, axis=-1, keepdims=True)
    centered = r - center
    variance = jnp.mean(centered * centered, axis=-1, keepdims=True)
    scale = lax.rsqrt(variance + NORM_EPS)
    return centered * scale, scale


def norm_back(dy, unit, scale, gain):
    du = dy * gain
    return scale * (
        du
        - jnp.mean(du, axis=-1, keepdims=True)
        - unit * jnp.mean(du * unit, axis=-1, keepdims=True)
    )


def load(refs, place_ref, parts, vmem, sem, down=False):
    for first, count, kind, unit, source, width, target in parts:
        j = 0
        for ref in refs[first : first + count]:
            for i in range(ref.shape[0]):
                start = pl.multiple_of(place_ref[kind, j], 16)
                j += 1
                for g in range(4 if down else 1):
                    columns = pl.ds(source + g * D, D) if down else pl.ds(source, width)
                    at = pl.ds(pl.multiple_of(start + 32 * g, 16), unit)
                    to = pl.ds(0, D) if down else pl.ds(target, width)
                    pltpu.make_async_copy(ref.at[i, :, columns], vmem.at[at, to], sem).start()


def unload(refs, place_ref, base, kind, vmem, sem):
    j = 0
    for ref in refs:
        for i in range(ref.shape[0]):
            start = pl.multiple_of(place_ref[kind, j], 16)
            j += 1
            for g in range(4 if kind else 1):
                at = pl.ds(pl.multiple_of(start + 32 * g, 16), WROWS)
                to = ref.at[i, :, pl.ds(base + g * D, D)] if kind else ref.at[i, :, pl.ds(base, vmem.shape[1])]
                pltpu.make_async_copy(vmem.at[at, :], to, sem).start()


def begin(source, target, sem):
    copy = pltpu.make_async_copy(source, target, sem)
    copy.start()
    return copy


def by_chunks(source, target, sems):
    return [begin(source.at[pl.ds(t * CH, CH), :], target.at[pl.ds(t * CH, CH), :], sems.at[t]) for t in range(NCH)]


def whole(vmem, sem):
    pltpu.make_async_copy(vmem, vmem, sem).wait()


def lane_of(shape):
    return lax.broadcasted_iota(jnp.int32, shape, len(shape) - 1)


def attend_kernel(first, parts, count, place_ref, x_hbm, vec_ref, kaug_hbm, qone_hbm, bias_hbm, *rest):
    refs = rest[:count]
    (
        xb_hbm, qkv_hbm, mixed_hbm, lse_hbm, mixed_ref, state_ref,
        x_ref, w, xb_ref, qkv_ref, lse_ref, kaug_ref, qone_ref, bias_ref, sem, sems, xsems,
    ) = rest[count:]
    states = by_chunks(x_hbm, x_ref, xsems)
    load(refs, place_ref, parts["qkv"], w, sem)
    masks = [
        begin(kaug_hbm, kaug_ref, sems.at[0]),
        begin(qone_hbm, qone_ref, sems.at[1]),
        begin(bias_hbm, bias_ref, sems.at[2]),
    ]
    for t in range(NCH):
        states[t].wait()
        x = x_ref[rows(t), :]
        if not first:
            x = normalize(x)[0] * vec_ref[0:1, :] + vec_ref[1:2, :]
        state_ref[rows(t), :] = x
        xb_ref[rows(t), :] = x.astype(BF16)
    lse_ref[...] = jnp.zeros((TILE, 128), F32)
    outs = [begin(xb_ref, xb_hbm, sems.at[3])]
    whole(w, sem)
    for t in range(NCH):
        qkv_ref[rows(t), :] = dn(xb_ref[rows(t), :], w[...]).astype(BF16)
    outs.append(begin(qkv_ref, qkv_hbm, sems.at[4]))
    for copy in masks:
        copy.wait()
    ones = jnp.ones((TILE, 128), BF16)
    lane = lane_of((CH, 128))

    def pair(hp, carry):
        at = pl.multiple_of(hp * 128, 128)
        keys = qkv_ref[:, pl.ds(D + at, 128)]
        full_keys = jnp.concatenate([keys, kaug_ref[...]], axis=1)
        full_values = jnp.concatenate([qkv_ref[:, pl.ds(2 * D + at, 128)], ones], axis=1)
        for t in range(NCH):
            queries = qkv_ref[rows(t), pl.ds(at, 128)] * jnp.asarray(0.125, BF16)
            outs = []
            for half in range(2):
                q = jnp.where((lane >= 64) == (half == 1), queries, jnp.zeros_like(queries))
                near = nt(q, keys[rows(t)]) + bias_ref[t]
                top = jnp.max(near, axis=-1, keepdims=True)
                if t:
                    far = nt(jnp.concatenate([q, qone_ref[rows(t), :]], axis=1), full_keys[: t * CH])
                    top = jnp.maximum(top, jnp.max(far, axis=-1, keepdims=True))
                    near = jnp.concatenate([far, near], axis=1)
                probs = jnp.exp(near - top).astype(BF16)
                o = dn(probs, full_values[: (t + 1) * CH])
                total = o[:, 128:]
                outs.append(o[:, :128] / total)
                here = ((lane & 7) == 2 * hp + half) & (lane < 24)
                lse_ref[rows(t), :] = jnp.where(here, top + jnp.log(total), lse_ref[rows(t), :])
            mixed_ref[rows(t), pl.ds(at, 128)] = jnp.where(lane < 64, outs[0], outs[1]).astype(BF16)
        return carry

    lax.fori_loop(0, HEADS // 2, pair, 0)
    outs.append(begin(mixed_ref, mixed_hbm, sems.at[5]))
    outs.append(begin(lse_ref, lse_hbm, sems.at[6]))
    for copy in outs:
        copy.wait()


def before_pairs(dr1_ref, mixed_ref, lse_ref, qone_ref, wo, dm, extra):
    wide = lane_of((D, 128))
    feature = lax.broadcasted_iota(jnp.int32, (D, 128), 0)
    collect = jnp.where(
        ((feature >> 6) == (wide & 7)) & (wide >= SUM_LANE) & (wide < SUM_LANE + 24), 1.0, 0.0
    ).astype(BF16)
    group = (lane_of((CH, 128)) >> 3) & 3
    for t in range(NCH):
        d = nt(dr1_ref[rows(t), :].astype(BF16), wo[...]).astype(BF16)
        dm[rows(t), :] = d
        prod = d.astype(F32) * mixed_ref[rows(t), :].astype(F32)
        high = prod.astype(BF16)
        low = (prod - high.astype(F32)).astype(BF16)
        v = lse_ref[rows(t), :] + dn(high, collect) + dn(low, collect)
        a = v.astype(BF16).astype(F32)
        b = (v - a).astype(BF16).astype(F32)
        c = v - a - b
        v = jnp.where(group == 0, a, jnp.where(group == 1, b, c))
        extra[rows(t), :] = (v + qone_ref[rows(t), :].astype(F32)).astype(BF16)


def back_pairs(start, count, qkv_ref, dm, extra, kaug_ref, bias_ref, dq, dqkv):
    one = lane_of((1, 128))
    alllane = lane_of((TILE, 128))
    width = count * 128

    def pair(i, carry):
        hp = i + start
        at = pl.multiple_of(hp * 128, 128)
        to = pl.multiple_of(i * 128, 128)
        queries = qkv_ref[:, pl.ds(at, 128)] * jnp.asarray(0.125, BF16)
        keys = qkv_ref[:, pl.ds(D + at, 128)]
        values = qkv_ref[:, pl.ds(2 * D + at, 128)]
        dmp = dm[:, pl.ds(at, 128)]
        full_q = jnp.concatenate([queries, extra[...]], axis=1)
        full_d = jnp.concatenate([dmp, extra[...]], axis=1)
        zero = jnp.zeros_like(queries)
        dks = [None] * NCH
        dvs = [None] * NCH
        for half in range(2):
            mine = (alllane >= 64) == (half == 1)
            h = 2 * hp + half
            q, k, v, g = (jnp.where(mine, a, zero) for a in (queries, keys, values, dmp))
            pick = (one & 7) == h
            sel_s = jnp.where(pick & (one < 24), -1.0, 0.0).astype(BF16)
            sel_d = jnp.where(pick & (one >= SUM_LANE) & (one < SUM_LANE + 24), -1.0, 0.0).astype(BF16)
            k8 = k * jnp.asarray(0.125, BF16)
            for c in range(NCH):
                near_k = jnp.concatenate([k[rows(c)], jnp.broadcast_to(sel_s, (CH, 128))], axis=1)
                s = nt(near_k, full_q[rows(c)]) + bias_ref[c]
                if c < NCH - 1:
                    far_k = jnp.concatenate([k[rows(c)], kaug_ref[rows(c), :] + sel_s], axis=1)
                    s = jnp.concatenate([s, nt(far_k, full_q[(c + 1) * CH :])], axis=1)
                p = jnp.exp(s)
                vf = jnp.concatenate([v[rows(c)], jnp.broadcast_to(sel_d, (CH, 128))], axis=1)
                ds = (p * nt(vf, full_d[c * CH :])).astype(BF16)
                dv = dn(p.astype(BF16), g[c * CH :])
                dk = dn(ds, q[c * CH :])
                dvs[c] = dv if half == 0 else dvs[c] + dv
                dks[c] = dk if half == 0 else dks[c] + dk
                part = tn(ds, k8[rows(c)])
                if half == 0 and c == 0:
                    dq[...] = part
                else:
                    dq[c * CH :, :] += part
        dqkv[:, pl.ds(to, 128)] = dq[...].astype(BF16)
        for c in range(NCH):
            dqkv[rows(c), pl.ds(width + to, 128)] = dks[c].astype(BF16)
            dqkv[rows(c), pl.ds(2 * width + to, 128)] = dvs[c].astype(BF16)
        return carry

    lax.fori_loop(0, count, pair, 0)


def take(hbm, vmem, sems, at, pairs=None):
    if pairs is None:
        return [begin(hbm, vmem, sems.at[at])]
    start, size = pairs
    copies = []
    for i in range(3):
        columns = pl.ds(i * D + start * 128, size * 128)
        copies.append(begin(hbm.at[:, columns], vmem.at[:, columns], sems.at[at + i]))
    return copies


def done(copies):
    for copy in copies:
        copy.wait()


def attend_back_kernel(parts, count, pairs, place_ref, gplace_ref, dr1_ref, *rest):
    mixed_hbm, qkv_hbm, lse_hbm, xb_hbm, kaug_hbm, qone_hbm, bias_hbm = rest[:7]
    refs, rest = rest[7 : 7 + count], rest[7 + count :]
    every = pairs == HEADS // 2
    if every:
        dx_hbm, keep_hbm, send_hbm, dm, extra, dqkv, dx_ref, dxsems, w, sem, dr1_v, dr1sem, *rest = rest
    else:
        dm, extra, dqkv_hbm, keep_hbm, send_hbm, dqkv, dsem, *rest = rest
    wo, dq, gw, mixed_ref, qkv_ref, lse_ref, xb_ref, kaug_ref, qone_ref, bias_ref, osem, gsem, sems = rest
    early = take(mixed_hbm, mixed_ref, sems, 0)
    if every:
        early.append(begin(dr1_ref, dr1_v, dr1sem))
        dr1_ref = dr1_v
    load(refs, place_ref, parts["wo"], wo, osem)
    middle = take(lse_hbm, lse_ref, sems, 1) + take(qone_hbm, qone_ref, sems, 2)
    late = (
        take(qkv_hbm, qkv_ref, sems, 3, (0, pairs))
        + take(kaug_hbm, kaug_ref, sems, 6)
        + take(bias_hbm, bias_ref, sems, 7)
    )
    last = take(xb_hbm, xb_ref, sems, 8)
    if every:
        load(refs, place_ref, parts["qkv"], w, sem)
    width = 3 * pairs * 128
    done(early)
    gw[:, width:] = tn(mixed_ref[...], dr1_ref[...].astype(BF16)).astype(BF16)
    whole(wo, osem)
    done(middle)
    before_pairs(dr1_ref, mixed_ref, lse_ref, qone_ref, wo, dm, extra)
    done(late)
    back_pairs(0, pairs, qkv_ref, dm, extra, kaug_ref, bias_ref, dq, dqkv)
    outs = [] if every else [begin(dqkv, dqkv_hbm, dsem)]
    done(last)
    gw[:, :width] = tn(xb_ref[...], dqkv[...]).astype(BF16)
    unload([keep_hbm, send_hbm], gplace_ref, 0, 0, gw, gsem)
    if every:
        whole(w, sem)
        for t in range(NCH):
            dx_ref[rows(t), :] = dr1_ref[rows(t), :] + nt(dqkv[rows(t), :], w[...])
            part = pl.ds(t * CH, CH)
            outs.append(begin(dx_ref.at[part, :], dx_hbm.at[part, :], dxsems.at[t]))
    whole(gw, gsem)
    done(outs)


def right_kernel(
    gplace_ref, dm, extra, qkv_hbm, xb_hbm, kaug_hbm, bias_hbm, dqkv_hbm, keep_hbm, send_hbm,
    dqkv, dq, gw, qkv_ref, xb_ref, kaug_ref, bias_ref, gsem, sems,
):
    pairs = HEADS // 4
    early = (
        take(qkv_hbm, qkv_ref, sems, 0, (pairs, pairs))
        + take(kaug_hbm, kaug_ref, sems, 3)
        + take(bias_hbm, bias_ref, sems, 4)
    )
    late = take(xb_hbm, xb_ref, sems, 5)
    done(early)
    back_pairs(pairs, pairs, qkv_ref, dm, extra, kaug_ref, bias_ref, dq, dqkv)
    out = begin(dqkv, dqkv_hbm, sems.at[6])
    done(late)
    gw[...] = tn(xb_ref[...], dqkv[...]).astype(BF16)
    unload([keep_hbm, send_hbm], gplace_ref, 0, 0, gw, gsem)
    whole(gw, gsem)
    out.wait()


def input_kernel(parts, count, place_ref, dr1_ref, left_hbm, right_hbm, chan_ref, *rest):
    refs = rest[:count]
    dx_hbm, dchan_ref, w, left_ref, right_ref, dx_ref, sem, sems, dxsems = rest[count:]
    load(refs, place_ref, parts["qkv"], w, sem)
    loads = [begin(left_hbm, left_ref, sems.at[0]), begin(right_hbm, right_ref, sems.at[1])]
    whole(w, sem)
    done(loads)
    outs = []
    half = D // 2
    for t in range(NCH):
        grads = [
            ref[rows(t), i * half : (i + 1) * half] for i in range(3) for ref in (left_ref, right_ref)
        ]
        dx = dr1_ref[rows(t), :] + nt(jnp.concatenate(grads, axis=1), w[...])
        dx_ref[rows(t), :] = dx.astype(BF16)
        part = pl.ds(t * CH, CH)
        outs.append(begin(dx_ref.at[part, :], dx_hbm.at[part, :], dxsems.at[t]))
        pick = chan_ref[:, rows(t)]
        a = dx.astype(BF16)
        b = (dx - a.astype(F32)).astype(BF16)
        c = (dx - a.astype(F32) - b.astype(F32)).astype(BF16)
        total = dn(pick, a) + dn(pick, b) + dn(pick, c)
        dchan_ref[...] = total if t == 0 else dchan_ref[...] + total
    done(outs)


def forward_kernel(last, parts, count, place_ref, x_ref, mixed_ref, vec_ref, *rest):
    refs = rest[:count]
    if last:
        r1_ref, r2_ref, wo, w, wd, osem, sem, dsem = rest[count:]
    else:
        r1_hbm, r2_hbm, wo, w, wd, r1_ref, r2_ref, osem, sem, dsem, sems = rest[count:]
    load(refs, place_ref, parts["wo"], wo, osem)
    load(refs, place_ref, parts["up"], w, sem)
    load(refs, place_ref, parts["down"], wd, dsem, True)
    whole(wo, osem)
    for t in range(NCH):
        r1 = x_ref[rows(t), :] + dn(mixed_ref[rows(t), :], wo[...])
        r1_ref[rows(t), :] = r1
        r2_ref[rows(t), :] = normalize(r1)[0] * vec_ref[0:1, :] + vec_ref[1:2, :]
    outs = [] if last else [begin(r1_ref, r1_hbm, sems.at[NCH])]
    whole(w, sem)
    whole(wd, dsem)
    for t in range(NCH):
        back = r2_ref[rows(t), :]
        hb = back.astype(BF16)
        for c in range(FF // D):
            x = dn(hb, w[:, c * D : (c + 1) * D])
            half = 0.5 * x
            act = half + half * jnp.tanh(x * (GELU_A + GELU_B * (x * x)))
            back = back + dn(act.astype(BF16), wd[c * D : (c + 1) * D, :])
        r2_ref[rows(t), :] = back
        if not last:
            part = pl.ds(t * CH, CH)
            outs.append(begin(r2_ref.at[part, :], r2_hbm.at[part, :], sems.at[t]))
    for copy in outs:
        copy.wait()


def back_kernel(
    last, parts, count, gcount, place_ref, gplace_ref, dy_ref, r2_ref, r1_ref, vec_ref, *rest,
):
    refs = rest[:count]
    g_hbm = rest[count : count + gcount]
    dr1_ref, dvec_ref, *rest = rest[count + gcount :]
    if last:
        out_ref, w, wd, dr2, db, hb, act, dpre, gw, gd, sem, dsem, gsem, gdsem = rest
    else:
        w, wd, dr2, db, hb, act, dpre, gw, gd, sem, dsem, gsem, gdsem, r2_v, r1_v, dy_v, sems = rest
        loads = [begin(r2_ref, r2_v, sems.at[0]), begin(dy_ref, dy_v, sems.at[1]), begin(r1_ref, r1_v, sems.at[2])]
        r2_ref, r1_ref, dy_ref = r2_v, r1_v, dy_v
    load(refs, place_ref, parts["up"], w, sem)
    load(refs, place_ref, parts["down"], wd, dsem, True)
    dgain = jnp.zeros((1, D), F32)
    dshift = jnp.zeros((1, D), F32)
    if not last:
        done(loads[:2])
    for t in range(NCH):
        unit, scale = normalize(r2_ref[rows(t), :])
        dy = dy_ref[rows(t), :].astype(F32)
        if last:
            out_ref[rows(t), :] = (unit * vec_ref[2:3, :] + vec_ref[3:4, :]).astype(BF16)
        dgain += jnp.sum(dy * unit, axis=0, keepdims=True)
        dshift += jnp.sum(dy, axis=0, keepdims=True)
        dr = norm_back(dy, unit, scale, vec_ref[2:3, :])
        dr2[rows(t), :] = dr
        db[rows(t), :] = dr.astype(BF16)
    if not last:
        loads[2].wait()
    for t in range(NCH):
        h = normalize(r1_ref[rows(t), :])[0] * vec_ref[0:1, :] + vec_ref[1:2, :]
        hb[rows(t), :] = h.astype(BF16)
    dvec_ref[2:3, :] = dgain
    dvec_ref[3:4, :] = dshift
    whole(w, sem)
    whole(wd, dsem)
    for t in range(NCH):
        for c in range(FF // D):
            cols = slice(c * D, (c + 1) * D)
            x = dn(hb[rows(t), :], w[:, cols])
            dact = nt(db[rows(t), :], wd[cols, :])
            half = 0.5 * x
            x2 = x * x
            th = jnp.tanh(x * (GELU_A + GELU_B * x2))
            act[rows(t), cols] = (half + half * th).astype(BF16)
            slope = (0.5 + 0.5 * th) + (half - half * (th * th)) * (GELU_A + 3 * GELU_B * x2)
            dp = (dact * slope).astype(BF16)
            dpre[rows(t), cols] = dp
            dr2[rows(t), :] += nt(dp, w[:, cols])
    for c in range(FF // D):
        cols = slice(c * D, (c + 1) * D)
        gd[cols, :] = tn(act[:, cols], db[...]).astype(BF16)
    unload(g_hbm if last else g_hbm[2:], gplace_ref, FF if last else 0, 1, gd, gdsem)
    for c in range(FF // D):
        cols = slice(c * D, (c + 1) * D)
        gw[:, cols] = tn(hb[...], dpre[:, cols]).astype(BF16)
    unload(g_hbm if last else g_hbm[:2], gplace_ref, 0, 0, gw, gsem)
    dgain = jnp.zeros((1, D), F32)
    dshift = jnp.zeros((1, D), F32)
    for t in range(NCH):
        unit, scale = normalize(r1_ref[rows(t), :])
        dy = dr2[rows(t), :]
        dgain += jnp.sum(dy * unit, axis=0, keepdims=True)
        dshift += jnp.sum(dy, axis=0, keepdims=True)
        dr1_ref[rows(t), :] = norm_back(dy, unit, scale, vec_ref[0:1, :])
    dvec_ref[0:1, :] = dgain
    dvec_ref[1:2, :] = dshift
    whole(gd, gdsem)
    whole(gw, gsem)


def turn_kernel(parts, count, place_ref, gplace_ref, x_ref, mixed_hbm, dy_ref, vec_ref, *rest):
    refs = rest[:count]
    (
        g_hbm, out_hbm, dr1_hbm, dvec_ref, wo, w, wd, r1_ref, slope, dr2, db, hb, act, dpre, gw, gd, out_ref,
        dr1_ref, mixed_ref, osem, sem, dsem, gsem, gdsem, outsems, dr1sems, msem,
    ) = rest[count:]
    loads = [begin(mixed_hbm, mixed_ref, msem)]
    load(refs, place_ref, parts["wo"], wo, osem)
    load(refs, place_ref, parts["up"], w, sem)
    load(refs, place_ref, parts["down"], wd, dsem, True)
    whole(wo, osem)
    done(loads)
    for t in range(NCH):
        r1_ref[rows(t), :] = x_ref[rows(t), :] + dn(mixed_ref[rows(t), :], wo[...])
    whole(w, sem)
    whole(wd, dsem)
    outs = []
    dgain = jnp.zeros((1, D), F32)
    dshift = jnp.zeros((1, D), F32)
    for t in range(NCH):
        back = normalize(r1_ref[rows(t), :])[0] * vec_ref[0:1, :] + vec_ref[1:2, :]
        low = back.astype(BF16)
        hb[rows(t), :] = low
        for c in range(FF // D):
            cols = slice(c * D, (c + 1) * D)
            x = dn(low, w[:, cols])
            half = 0.5 * x
            x2 = x * x
            th = jnp.tanh(x * (GELU_A + GELU_B * x2))
            a = (half + half * th).astype(BF16)
            act[rows(t), cols] = a
            slope[:, cols] = (0.5 + 0.5 * th) + (half - half * (th * th)) * (GELU_A + 3 * GELU_B * x2)
            back = back + dn(a, wd[cols, :])
        unit, scale = normalize(back)
        dy = dy_ref[rows(t), :].astype(F32)
        out_ref[rows(t), :] = (unit * vec_ref[2:3, :] + vec_ref[3:4, :]).astype(BF16)
        part = pl.ds(t * CH, CH)
        outs.append(begin(out_ref.at[part, :], out_hbm.at[part, :], outsems.at[t]))
        dgain += jnp.sum(dy * unit, axis=0, keepdims=True)
        dshift += jnp.sum(dy, axis=0, keepdims=True)
        dr = norm_back(dy, unit, scale, vec_ref[2:3, :])
        low = dr.astype(BF16)
        db[rows(t), :] = low
        for c in range(FF // D):
            cols = slice(c * D, (c + 1) * D)
            dp = (nt(low, wd[cols, :]) * slope[:, cols]).astype(BF16)
            dpre[rows(t), cols] = dp
            dr = dr + nt(dp, w[:, cols])
        dr2[rows(t), :] = dr
    dvec_ref[2:3, :] = dgain
    dvec_ref[3:4, :] = dshift
    for c in range(FF // D):
        cols = slice(c * D, (c + 1) * D)
        gd[cols, :] = tn(act[:, cols], db[...]).astype(BF16)
    unload([g_hbm], gplace_ref, FF, 1, gd, gdsem)
    for c in range(FF // D):
        cols = slice(c * D, (c + 1) * D)
        gw[:, cols] = tn(hb[...], dpre[:, cols]).astype(BF16)
    unload([g_hbm], gplace_ref, 0, 0, gw, gsem)
    dgain = jnp.zeros((1, D), F32)
    dshift = jnp.zeros((1, D), F32)
    for t in range(NCH):
        unit, scale = normalize(r1_ref[rows(t), :])
        dy = dr2[rows(t), :]
        dgain += jnp.sum(dy * unit, axis=0, keepdims=True)
        dshift += jnp.sum(dy, axis=0, keepdims=True)
        dr1_ref[rows(t), :] = norm_back(dy, unit, scale, vec_ref[0:1, :])
        part = pl.ds(t * CH, CH)
        outs.append(begin(dr1_ref.at[part, :], dr1_hbm.at[part, :], dr1sems.at[t]))
    dvec_ref[0:1, :] = dgain
    dvec_ref[1:2, :] = dshift
    whole(gd, gdsem)
    whole(gw, gsem)
    done(outs)


def sds(shape, dtype=F32):
    return jax.ShapeDtypeStruct(shape, dtype)


KEPT = "kept"


def call(kernel, name, us, mib, outs, in_specs, out_specs, scratch, aliases=None):
    spaces = {id(KEPT): pltpu.VMEM, id(ANY): pltpu.HBM}

    def kept(shape, spec):
        space = spaces.get(id(spec))
        return space(shape.shape, shape.dtype) if space else shape

    def run(*args):
        args = [
            pltpu.with_memory_space_constraint(a, spaces[id(s)]) if id(s) in spaces else a
            for a, s in zip(args, in_specs)
        ]
        return pl.pallas_call(
            kernel,
            out_shape=[kept(o, s) for o, s in zip(outs, out_specs)],
            in_specs=[VMEM if s is KEPT else s for s in in_specs],
            out_specs=[VMEM if s is KEPT else s for s in out_specs],
            scratch_shapes=scratch,
            input_output_aliases=aliases or {},
            compiler_params=pltpu.CompilerParams(vmem_limit_bytes=mib * 1024 * 1024),
            cost_estimate=pl.CostEstimate(flops=us * 400000000, transcendentals=0, bytes_accessed=us * 1200000),
            name=name,
        )(*args)

    return run


DMA = pltpu.SemaphoreType.DMA


def mask_scratch():
    return [pltpu.VMEM((TILE, 128), BF16), pltpu.VMEM((TILE, 128), BF16), pltpu.VMEM((NCH, CH, CH), F32)]


def attend(level, x, vec, masks, weights):
    kaug, qone, bias, _ = masks
    place, parts, bufs = weights
    return call(
        functools.partial(attend_kernel, level == 0, parts, len(bufs)),
        f"attend{level}",
        18,
        28,
        [sds((TILE, D), BF16), sds((TILE, 3 * D), BF16), sds((TILE, D), BF16), sds((TILE, 128))]
        + [sds((TILE, D), BF16), sds((TILE, D))],
        [SMEM, ANY, VMEM] + [ANY] * (3 + len(bufs)),
        [ANY] * 4 + [KEPT] * 2,
        [
            pltpu.VMEM((TILE, D), F32),
            pltpu.VMEM((D, 3 * D), BF16),
            pltpu.VMEM((TILE, D), BF16),
            pltpu.VMEM((TILE, 3 * D), BF16),
            pltpu.VMEM((TILE, 128), F32),
            *mask_scratch(),
            DMA,
            pltpu.SemaphoreType.DMA((7,)),
            pltpu.SemaphoreType.DMA((NCH,)),
        ],
    )(place, x, vec, kaug, qone, bias, *bufs)


def grad_pair(columns):
    return [sds((KB // 2, WROWS, columns), BF16)] * 2


def attend_back(dr1, kept, masks, weights, gplace, pairs=HEADS // 2):
    kaug, qone, _, bias = masks
    place, parts, bufs = weights
    xb, qkv, mixed, lse = kept
    every = pairs == HEADS // 2
    width = 3 * pairs * 128
    pieces = grad_pair(width + D)
    own = [sds((TILE, D), BF16), sds((TILE, 128), BF16), sds((TILE, width), BF16)]
    if every:
        scratch = [pltpu.VMEM(o.shape, o.dtype) for o in own]
        scratch += [pltpu.VMEM((TILE, D), F32), pltpu.SemaphoreType.DMA((NCH,)), pltpu.VMEM((D, 3 * D), BF16), DMA]
        scratch += [pltpu.VMEM((TILE, D), F32), DMA]
    else:
        scratch = [pltpu.VMEM((TILE, width), BF16), DMA]
    return call(
        functools.partial(attend_back_kernel, parts, len(bufs), pairs),
        "attend_back" if every else "attend_left",
        28 if every else 17,
        36 if every else 28,
        [sds((TILE, D))] + pieces if every else own + pieces,
        [SMEM] * 2 + [ANY if every else KEPT] + [ANY] * (7 + len(bufs)),
        ([ANY] if every else [KEPT, KEPT, ANY]) + [ANY] * 2,
        scratch
        + [
            pltpu.VMEM((D, D), BF16),
            pltpu.VMEM((TILE, 128), F32),
            pltpu.VMEM((D, width + D), BF16),
            pltpu.VMEM((TILE, D), BF16),
            pltpu.VMEM((TILE, 3 * D), BF16),
            pltpu.VMEM((TILE, 128), F32),
            pltpu.VMEM((TILE, D), BF16),
            *mask_scratch(),
            DMA,
            DMA,
            pltpu.SemaphoreType.DMA((9,)),
        ],
    )(place, gplace, dr1, mixed, qkv, lse, xb, kaug, qone, bias, *bufs)


def attend_left(dr1, kept, masks, weights, gplace):
    return attend_back(dr1, kept, masks, weights, gplace, HEADS // 4)


def attend_right(dm, extra, kept, masks, gplace):
    kaug, _, _, bias = masks
    xb, qkv = kept[:2]
    scratch = mask_scratch()
    return call(
        right_kernel,
        "attend_right",
        14,
        24,
        [sds((TILE, 3 * D // 2), BF16)] + grad_pair(3 * D // 2),
        [SMEM, KEPT, KEPT] + [ANY] * 4,
        [ANY, ANY, ANY],
        [
            pltpu.VMEM((TILE, 3 * D // 2), BF16),
            pltpu.VMEM((TILE, 128), F32),
            pltpu.VMEM((D, 3 * D // 2), BF16),
            pltpu.VMEM((TILE, 3 * D), BF16),
            pltpu.VMEM((TILE, D), BF16),
            scratch[0],
            scratch[2],
            DMA,
            pltpu.SemaphoreType.DMA((7,)),
        ],
    )(gplace, dm, extra, qkv, xb, kaug, bias)


def input_grad(dr1, left, right, chan, weights):
    place, parts, bufs = weights
    return call(
        functools.partial(input_kernel, parts, len(bufs)),
        "input_grad",
        30,
        20,
        [sds((TILE, D), BF16), sds((8, D))],
        [SMEM, KEPT, ANY, ANY, VMEM] + [ANY] * len(bufs),
        [ANY, VMEM],
        [
            pltpu.VMEM((D, 3 * D), BF16),
            pltpu.VMEM((TILE, 3 * D // 2), BF16),
            pltpu.VMEM((TILE, 3 * D // 2), BF16),
            pltpu.VMEM((TILE, D), BF16),
            DMA,
            pltpu.SemaphoreType.DMA((2,)),
            pltpu.SemaphoreType.DMA((NCH,)),
        ],
    )(place, dr1, left, right, chan, *bufs)


def forward(level, x, mixed, vec, weights):
    place, parts, bufs = weights
    last = level == LAYERS - 1
    state = sds((TILE, D))
    return call(
        functools.partial(forward_kernel, last, parts, len(bufs)),
        f"forward{level}",
        13,
        26,
        [state] * 2,
        [SMEM, KEPT, KEPT, VMEM] + [ANY] * len(bufs),
        [KEPT] * 2 if last else [ANY] * 2,
        [pltpu.VMEM((D, D), BF16), pltpu.VMEM((D, FF), BF16), pltpu.VMEM((FF, D), BF16)]
        + ([] if last else [pltpu.VMEM((TILE, D), F32)] * 2)
        + [DMA] * 3
        + ([] if last else [pltpu.SemaphoreType.DMA((NCH + 1,))]),
    )(place, x, mixed, vec, *bufs)


def back(level, dy, r2, r1, vec, weights, gplace):
    place, parts, bufs = weights
    last = level == LAYERS - 1
    grads = [sds((KB, WROWS, 2 * FF), BF16)] if last else grad_pair(FF) * 2
    split = len(grads)
    outs = grads + [sds((TILE, D)), sds((4, D))]
    specs = [ANY] * split + [KEPT, VMEM]
    if last:
        outs.append(sds((TILE, D), BF16))
        specs.append(VMEM)
    got = call(
        functools.partial(back_kernel, last, parts, len(bufs), split),
        f"back{level}",
        24,
        42,
        outs,
        [SMEM] * 2 + [VMEM if last else ANY] + [KEPT if last else ANY] * 2 + [VMEM] + [ANY] * len(bufs),
        specs,
        [
            pltpu.VMEM((D, FF), BF16),
            pltpu.VMEM((FF, D), BF16),
            pltpu.VMEM((TILE, D), F32),
            pltpu.VMEM((TILE, D), BF16),
            pltpu.VMEM((TILE, D), BF16),
            pltpu.VMEM((TILE, FF), BF16),
            pltpu.VMEM((TILE, FF), BF16),
            pltpu.VMEM((D, FF), BF16),
            pltpu.VMEM((FF, D), BF16),
            DMA,
            DMA,
            DMA,
            DMA,
        ]
        + ([] if last else [pltpu.VMEM((TILE, D), F32)] * 3 + [pltpu.SemaphoreType.DMA((3,))]),
    )(place, gplace, dy, r2, r1, vec, *bufs)
    return got[:split], *got[split:]


def turn(x, mixed, dy, vec, weights, gplace):
    place, parts, bufs = weights
    return call(
        functools.partial(turn_kernel, parts, len(bufs)),
        "turn",
        30,
        42,
        [sds((KB, WROWS, 2 * FF), BF16), sds((TILE, D), BF16), sds((TILE, D)), sds((4, D))],
        [SMEM] * 2 + [KEPT, ANY, VMEM, VMEM] + [ANY] * len(bufs),
        [ANY, ANY, ANY, VMEM],
        [
            pltpu.VMEM((D, D), BF16),
            pltpu.VMEM((D, FF), BF16),
            pltpu.VMEM((FF, D), BF16),
            pltpu.VMEM((TILE, D), F32),
            pltpu.VMEM((CH, FF), F32),
            pltpu.VMEM((TILE, D), F32),
            pltpu.VMEM((TILE, D), BF16),
            pltpu.VMEM((TILE, D), BF16),
            pltpu.VMEM((TILE, FF), BF16),
            pltpu.VMEM((TILE, FF), BF16),
            pltpu.VMEM((D, FF), BF16),
            pltpu.VMEM((FF, D), BF16),
            pltpu.VMEM((TILE, D), BF16),
            pltpu.VMEM((TILE, D), F32),
            pltpu.VMEM((TILE, D), BF16),
            DMA,
            DMA,
            DMA,
            DMA,
            DMA,
            pltpu.SemaphoreType.DMA((NCH,)),
            pltpu.SemaphoreType.DMA((NCH,)),
            DMA,
        ],
    )(place, gplace, x, mixed, dy, vec, *bufs)


def adamw(weight, grad, first, second, rate):
    first_new = FIRST_DECAY * first + (1.0 - FIRST_DECAY) * grad
    second_new = SECOND_DECAY * second + (1.0 - SECOND_DECAY) * grad * grad
    first_fix = 1.0 - FIRST_DECAY**STEP
    second_fix = 1.0 - SECOND_DECAY**STEP
    update = (
        first_new / first_fix / (jnp.sqrt(second_new / second_fix) + ADAM_EPS)
        + WEIGHT_DECAY * weight
    )
    return (weight - rate * update, first_new, second_new)


def update_kernel(dp_ref, main_ref, other_ref, right_ref, got_ref, *rest):
    states, rest = rest[:6], rest[14:]
    outs, (wide, down, loads, stores) = rest[:8], (rest[8:12], rest[12:16], rest[16], rest[17])
    copies = [
        begin(a.at[0], b, loads.at[i]) for i, (a, b) in enumerate(zip(states, (*wide[:3], *down[:3])))
    ]
    half = D // 2

    def step(held, place, grad):
        w, m, v, low = held
        new, first, second = adamw(w[place], grad, m[place], v[place], MATRIX_RATE)
        w[place], m[place], v[place], low[place] = new, first, second, new.astype(BF16)

    def columns(start, size):
        return slice(0, WROWS), slice(start, start + size)

    done(copies)
    for i in range(2):
        part = jnp.where(dp_ref[0] == i, main_ref[:, :FF].astype(F32), other_ref[:, :FF].astype(F32))
        step(wide, columns(4 * D + i * FF // 2, FF // 2), part[:, : FF // 2])
        for g in range(2):
            at = (2 * i + g) * WROWS
            step(down, (slice(at, at + WROWS), slice(0, D)), part[:, FF // 2 + g * D : FF // 2 + (g + 1) * D])
    lefts = [(FF + i * half, i * D, half) for i in range(3)] + [(FF + 3 * half, 3 * D, D)]
    rights = [(i * half, i * D + half, half) for i in range(3)]
    for pieces, mine, theirs in ((lefts, main_ref, other_ref), (rights, right_ref, got_ref)):
        for source, target, size in pieces:
            at = slice(source, source + size)
            step(wide, columns(target, size), mine[:, at].astype(F32) + theirs[:, at].astype(F32))
    done([begin(b, a.at[0], stores.at[i]) for i, (a, b) in enumerate(zip(outs, (*wide, *down)))])


def update_first(dp, main, other, right, got, states, results):
    def held(rows_, columns):
        return [pltpu.VMEM((rows_, columns), F32)] * 3 + [pltpu.VMEM((rows_, columns), BF16)]

    return call(
        update_kernel,
        "update",
        3,
        12,
        [sds(r.shape, r.dtype) for r in results],
        [SMEM] + [VMEM] * 4 + [ANY] * 14,
        [ANY] * 8,
        held(WROWS, 4 * D + FF) + held(DROWS, D) + [pltpu.SemaphoreType.DMA((6,)), pltpu.SemaphoreType.DMA((8,))],
        {11 + i: i for i in range(8)},
    )(dp.reshape(1), main, other, right, got, *states, *results)


def mask_arrays(valid_count, table):
    places = jnp.arange(TILE, dtype=jnp.int32)
    block = (places >> 9) * 2 + ((places >> 5) & 1)
    member = block[:, None] == jnp.arange(NBLK, dtype=jnp.int32)[None, :]
    open_to = jnp.any(member[:, None, :] & (table[None] == 1), axis=-1) & (places < valid_count)[:, None]
    penalty = jnp.where(open_to, 0.0, MASKED_SCORE).astype(F32)
    pads = ((0, 0), (BLOCK_LANE, 128 - BLOCK_LANE - NBLK))
    kaug = jnp.pad(penalty, pads).astype(BF16)
    qone = jnp.pad(member.astype(F32), pads).astype(BF16)
    near = jnp.arange(CH, dtype=jnp.int32)
    visible = jnp.any(
        member.reshape(NCH, CH, 1, NBLK) & open_to.reshape(NCH, 1, CH, NBLK), axis=-1
    ) & (near[None, :] <= near[:, None])
    visible = visible | (near[None, :] == near[:, None])
    bias = jnp.where(visible, 0.0, MASKED_SCORE).astype(F32)
    return kaug, qone, bias, bias.transpose(0, 2, 1)


def pick_rows(order, size):
    n = order.shape[0]
    place = (order[:, None] * size + jnp.arange(size, dtype=jnp.int32)[None, :]).reshape(-1)
    return (place[None, :] == jnp.arange(n * size, dtype=jnp.int32)[:, None]).astype(BF16)


def pack_down(down):
    lead = down.shape[:-2]
    return jnp.swapaxes(down.reshape(*lead, 4, WROWS, D), -3, -2).reshape(*lead, WROWS, FF)


def unpack_down(packed):
    lead = packed.shape[:-2]
    return jnp.swapaxes(packed.reshape(*lead, WROWS, 4, D), -3, -2).reshape(*lead, DROWS, D)


def swap(v, bit):
    n = lax.axis_size("fsdp")
    return lax.ppermute(v, "fsdp", [(i, i ^ bit) for i in range(n)])


def swap_dp(v):
    return lax.ppermute(v, "dp", [(0, 1), (1, 0)])


def add(a, b):
    return (a.astype(F32) + b.astype(F32)).astype(BF16)


def together(*values):
    return lax.optimization_barrier(values)


def z_stage(shard):
    return jnp.concatenate([shard] + [swap(shard, 4 * k) for k in (1, 2, 3)], axis=0)


def axis_stage(pieces, cut):
    left, right = pieces[:, :, :cut], pieces[:, :, cut:]
    return (
        jnp.concatenate([left, swap(left, 2)], axis=0),
        jnp.concatenate([right, swap_dp(right)], axis=0),
    )


def cross_stage(left, right):
    return swap_dp(left), swap(right, 2)


def core_stage(left, right, left2, right2):
    left, right = [left, left2], [right, right2]
    return [*left, *(swap(a, 1) for a in left), *right, *(swap(a, 1) for a in right)]


def halves(keep, got):
    m = keep.shape[0] // 2
    return add(keep[:m], got[:m]), add(keep[m:], got[m:])


def dp_halves(dp, keep, got):
    m = keep.shape[2] // 2
    def side(i):
        return add(lax.dynamic_slice_in_dim(keep, i * m, m, 2), lax.dynamic_slice_in_dim(got, i * m, m, 2))
    return side(dp), side(1 - dp)


def stage(keep, move, send):
    return halves(keep, move(send))


def over_x(keep, send):
    return stage(keep, lambda a: swap(a, 2), send)


def over_z1(keep, send):
    return stage(keep, lambda a: swap(a, 4), send)


def over_z2(keep, send):
    return add(keep, swap(send, 8))[0]


def both(part):
    part = lax.reduce_precision(part.astype(F32), 8, 7)
    return part + swap_dp(part.astype(BF16)).astype(F32)


def split_halves(part):
    m = part.shape[0] // 2
    return part[:m], part[m:]


def with_vector(keep, send, v, move):
    high = lax.reduce_precision(v, 8, 7)
    low = lax.reduce_precision(v - high, 8, 7)
    block = jnp.pad(jnp.concatenate([high, low], axis=0).astype(BF16), ((0, 10), (0, send.shape[2] - D)))
    got = move(jnp.concatenate([send, block[None]], axis=0))
    part = got[0] if keep is None else add(keep, got[:-1])
    there = got[-1, :22, :D].astype(F32)
    return part, (high + low) + (there[:11] + there[11:])


def vector_step(v, move):
    high = lax.reduce_precision(v, 8, 7)
    low = lax.reduce_precision(v - high, 8, 7)
    got = move(jnp.concatenate([high, low], axis=0).astype(BF16)).astype(F32)
    return (high + low) + (got[: v.shape[0]] + got[v.shape[0] :])


def on_device(
    tokens, cotangent, key_valid, block_mask, row_owner, w_wide, w_down, gains, shifts,
    m_wide, v_wide, m_down, v_down, m_gain, v_gain, m_shift, v_shift,
):
    n = lax.axis_size("fsdp")
    direct = n == KB
    masks = mask_arrays(key_valid[0], block_mask[0])
    channel = jnp.arange(TILE, dtype=jnp.int32) % 3
    chan = (channel[None, :] == jnp.arange(8, dtype=jnp.int32)[:, None]).astype(BF16)
    embed = jnp.where(
        channel[:, None] == 0,
        shifts[2 * LAYERS],
        jnp.where(channel[:, None] == 1, shifts[2 * LAYERS + 1], shifts[2 * LAYERS + 2]),
    )
    x0 = tokens.astype(F32) + embed

    def places(order):
        return jnp.stack([order * WROWS, order * DROWS])

    def stored_places(order):
        return jnp.pad(places(order), ((3, 0), (0, KB)))

    ff_parts = {
        "wo": [(0, 1, 3, 32, 0, D, 0)],
        "up": [(0, 1, 3, 32, D, FF, 0)],
        "down": [(0, 1, 4, 32, D + FF, D, 0)],
    }
    if direct:
        me = lax.axis_index("fsdp")
        dp = lax.axis_index("dp")
        order = [row_owner[l] for l in range(LAYERS)]

        def owner_of(level, who):
            return jnp.sum(jnp.where(who[:, None] == jnp.arange(n, dtype=jnp.int32)[None, :], order[level][None, :], 0), axis=1)

        def near_places(level, names, size):
            axes = jnp.meshgrid(*(jnp.arange(4 if k == "z" else 2, dtype=jnp.int32) for k in names), indexing="ij")
            at = {k: a.reshape(-1) for k, a in zip(names, axes)}
            own = owner_of(level, me ^ (at["c"] + 2 * at["x"] + 4 * at["z"]))
            return own * size + (dp ^ at["d"]) * 16

        all_places = [
            jnp.concatenate(
                [
                    jnp.stack(
                        [near_places(l, "cdxz", WROWS), near_places(l, "cxdz", WROWS), near_places(l, "cxdz", DROWS)]
                    ),
                    jnp.pad(places(order[l]), ((0, 0), (0, KB))),
                ]
            )
            for l in range(LAYERS)
        ]
        half = 3 * D // 2
        att_parts = [
            {"qkv": [(0, 4, 0, 16, 0, half, 0), (4, 4, 1, 16, 0, half, half)]},
            {"qkv": [(0, 4, 0, 16, 0, 3 * D, 0)]},
        ]
        all_parts = [
            att_parts[0] | {"wo": [(8, 1, 3, 32, 0, D, 0)]},
            att_parts[1] | {"wo": [(0, 4, 0, 16, 3 * D, D, 0)]},
        ]
        ff_parts1 = {
            "wo": [(0, 4, 0, 16, 3 * D, D, 0)],
            "up": [(8, 1, 3, 32, 0, FF, 0)],
            "down": [(4, 4, 2, 16, 0, D, 0)],
        }
        low = [w_wide[l][:, 3 * D :].astype(BF16) for l in range(LAYERS)]
        packed_down = [pack_down(w_down[l].astype(BF16)) for l in range(LAYERS)]
        far = [
            lax.all_gather(a, "fsdp", axis=0)
            for a in (jnp.concatenate([low[0], packed_down[0]], axis=1), low[1][:, D:])
        ]
        mine = [
            lax.dynamic_slice_in_dim(a, dp * 16, 16, 0)[None]
            for a in (
                w_wide[0][:, : 3 * D].astype(BF16),
                jnp.concatenate([w_wide[1][:, : 4 * D].astype(BF16), packed_down[1]], axis=1),
            )
        ]
        piece = jnp.arange(KB, dtype=jnp.int32)
        relative = me ^ (piece // 8 + 2 * ((piece // 4) % 2) + 4 * ((piece // 2) % 2) + 8 * (piece % 2))
        stored1 = places(order[1])
        relative0, relative1 = (places(owner_of(l, relative)) for l in range(LAYERS))
    else:
        att_weights = []
        natural = places(jnp.arange(KB, dtype=jnp.int32))
        all_parts = {k: [(0, 1, i, r, c + 3 * D, w, 0) for _, _, i, r, c, w, _ in v] for k, v in ff_parts.items()}
        all_parts["qkv"] = [(0, 1, 3, 32, 0, 3 * D, 0)]
        for l in range(LAYERS):
            wide = lax.all_gather(w_wide[l].astype(BF16), "fsdp", axis=0, tiled=True)
            down = lax.all_gather(w_down[l].astype(BF16), "fsdp", axis=0, tiled=True)
            wide = dn(pick_rows(row_owner[l], D // n), wide).astype(BF16).reshape(KB, WROWS, 4 * D + FF)
            down = dn(pick_rows(row_owner[l], FF // n), down).astype(BF16).reshape(KB, DROWS, D)
            full = jnp.concatenate([wide, pack_down(down)], axis=2)
            att_weights.append((stored_places(jnp.arange(KB, dtype=jnp.int32)), all_parts, [full]))
        ff_weights = att_weights

    def sum_stored(level, full):
        pick = pick_rows(row_owner[level], full.shape[0] // n)
        part = lax.psum_scatter(tn(pick, full).astype(BF16), "fsdp", scatter_dimension=0, tiled=True)
        return both(part)

    def sum_ff(level, grad):
        if level:
            up, down = grad[..., :FF], grad[..., FF:]
        else:
            up, down = jnp.concatenate(grad[:2], axis=0), jnp.concatenate(grad[2:], axis=0)
        return sum_stored(level, up.reshape(D, FF)), sum_stored(level, unpack_down(down).reshape(FF, D))

    vecs = [
        jnp.stack([gains[2 * l], shifts[2 * l], gains[2 * l + 1], shifts[2 * l + 1]])
        for l in range(LAYERS)
    ]
    def forward_of(level, att, weights):
        *kept, mixed, x = att
        r1, r2 = forward(level, x, mixed, vecs[level], weights)
        return kept, r1, r2

    if direct:
        left, right, rest = together(*axis_stage(z_stage(mine[0]), half), mine[1])
        rest = z_stage(rest)
        left, right, left2, right2 = together(left, right, *cross_stage(left, right))
        near0 = core_stage(left, right, left2, right2)
        state, rest, *near0 = together(x0, rest, *near0)
        sides = axis_stage(rest, 4 * D)
        got = list(attend(0, state, vecs[0][0:2], masks, (all_places[0], att_parts[0], near0)))
        got[5], *sides = together(got[5], *sides)
        cross = cross_stage(*sides)
        kept0, r1_0, r2_0 = forward_of(0, got, (all_places[0], ff_parts, far[:1]))
        r2_0, *sides = together(r2_0, *sides, *cross)
        near1 = core_stage(*sides)
        got = attend(1, r2_0, vecs[0][2:4], masks, (all_places[1], att_parts[1], near1[:4]))
        ff_weights = [(all_places[0], ff_parts, far[:1]), (all_places[1], ff_parts1, near1 + far[1:])]
        back_weights = [
            (all_places[0], all_parts[0], near0 + far[:1]),
            (all_places[1], all_parts[1], near1[:4]),
        ]
    else:
        got = attend(0, x0, vecs[0][0:2], masks, att_weights[0])
        kept0, r1_0, r2_0 = forward_of(0, got, ff_weights[0])
        got = attend(1, r2_0, vecs[0][2:4], masks, att_weights[1])
    *kept1, _, x = got
    ff1, out_tokens, dr1, dvec1 = turn(
        x, kept1[2], cotangent, vecs[1], ff_weights[1], stored1 if direct else natural
    )
    if direct:
        ff1 = lax.psum_scatter(ff1, "fsdp", scatter_dimension=0)
        dx, *att1 = attend_back(dr1, kept1, masks, back_weights[1], relative1)
        dx, *att1 = together(dx, *att1)
        got1 = swap(att1[1], 1)
        ff0, dr1, dvec0 = back(0, dx, r2_0, r1_0, vecs[0], ff_weights[0], relative0)
        dr1, *work = together(dr1, *ff0, *halves(att1[0], got1))
        ff0, att1 = work[:4], work[4:]
        gotu = swap(ff0[1], 1)
        gotd = swap(ff0[3], 1)
        got1 = swap(att1[1], 2)
        dm, extra, dleft, *left = attend_left(dr1, kept0, masks, back_weights[0], relative0)
        extra, upk, ups, dok, dos, *work = together(
            extra, *halves(ff0[0], gotu), *dp_halves(dp, ff0[2], gotd), *left, *halves(att1[0], got1),
        )
        left, att1 = work[:2], work[2:]
        gotu = swap(ups, 2)
        gotd = swap_dp(dos)
        gotl = swap(left[1], 1)
        got1 = swap(att1[1], 4)
        dright, *right = attend_right(dm, extra, kept0, masks, relative0)
        dright, upk, ups, dok, dos, *work = together(
            dright, *dp_halves(dp, upk, gotu), *halves(dok, gotd), *halves(left[0], gotl), *right,
            *halves(att1[0], got1), ff1,
        )
        left, right, att1, ff1 = work[:2], work[2:4], work[4:6], work[6]
        gotu = swap_dp(ups)
        gotd = swap(dos, 2)
        gotl = swap(left[1], 2)
        gotr = swap(right[1], 1)
        got1 = swap(att1[1], 8)
        grad_tokens, dchan = input_grad(dr1, dleft, dright, chan, (all_places[0], att_parts[0], near0))
        att1 = add(att1[0], got1)[0]
        main = [jnp.concatenate(a, axis=2) for a in zip(halves(upk, gotu), halves(dok, gotd), halves(left[0], gotl))]
        keep, send, keepr, sendr, dchan, att1, ff1 = together(*main, *halves(right[0], gotr), dchan, att1, ff1)
        dvecs = jnp.concatenate([dvec0, dvec1], axis=0)
        vec = jnp.concatenate([dvecs[0::2], dvecs[1::2], dchan[:3]], axis=0)
        right, vec = with_vector(keepr, sendr, vec, lambda a: swap(a, 2))
        ff1 = both(ff1)
        keep, send, keepr, sendr, vec, att1, ff1 = together(
            *over_z1(keep, send), *split_halves(right), vec, att1, ff1
        )
        right, vec = with_vector(keepr, sendr, vec, lambda a: swap(a, 4))
        att1 = both(att1)
        main, keepr, sendr, vec, att1 = together(over_z2(keep, send), *split_halves(right), vec, att1)
        right, vec = with_vector(keepr, sendr, vec, lambda a: swap(a, 8))
        other, right, vec = together(swap_dp(main), right[0], vec)
        got, vec = with_vector(None, right[None], vec, swap_dp)
        vector_grad = vector_step(vec, lambda a: swap(a, 1))
        ups = [jnp.zeros((WROWS, FF), F32), ff1[:, :FF]]
        down_grads = [jnp.zeros((DROWS, D), F32), unpack_down(ff1[:, FF:])]
        atts = [jnp.zeros((WROWS, 4 * D), F32), att1]
    else:
        dx, *att1 = attend_back(dr1, kept1, masks, att_weights[1], natural)
        ff0, dr1, dvec0 = back(0, dx, r2_0, r1_0, vecs[0], ff_weights[0], natural)
        dm, extra, dleft, *left = attend_left(dr1, kept0, masks, att_weights[0], natural)
        dright, *right = attend_right(dm, extra, kept0, masks, natural)
        grad_tokens, dchan = input_grad(dr1, dleft, dright, chan, att_weights[0])
        ups, down_grads = zip(sum_ff(0, ff0), sum_ff(1, ff1))
        left, right = (jnp.concatenate(a, axis=0).reshape(D, -1) for a in (left, right))
        half = D // 2
        att0 = [a[:, i * half : (i + 1) * half] for i in range(3) for a in (left, right)]
        att0 = jnp.concatenate([*att0, left[:, 3 * half :]], axis=1)
        dvecs = jnp.concatenate([dvec0, dvec1], axis=0)
        vec = jnp.concatenate([dvecs[0::2], dvecs[1::2], dchan[:3]], axis=0)
        vector_grad = lax.psum(vec, ("fsdp", "dp"))
        atts = [sum_stored(0, att0), sum_stored(1, jnp.concatenate(att1, axis=0).reshape(D, 4 * D))]
    wide_grads = [jnp.concatenate([atts[l], ups[l]], axis=1) for l in range(LAYERS)]
    grad_gain, grad_shift = vector_grad[: 2 * LAYERS], vector_grad[2 * LAYERS :]
    grad_wide = jnp.stack(wide_grads)
    grad_down = jnp.stack(down_grads)
    new_wide, first_wide, second_wide = adamw(w_wide, grad_wide, m_wide, v_wide, MATRIX_RATE)
    new_down, first_down, second_down = adamw(w_down, grad_down, m_down, v_down, MATRIX_RATE)
    low_wide, low_down = new_wide.astype(BF16), new_down.astype(BF16)
    if direct:
        (
            new_wide, first_wide, second_wide, low_wide, new_down, first_down, second_down, low_down
        ) = update_first(
            dp, main, other, right, got,
            (w_wide, m_wide, v_wide, w_down, m_down, v_down),
            (new_wide, first_wide, second_wide, low_wide, new_down, first_down, second_down, low_down),
        )
    new_gains, first_gain, second_gain = adamw(gains, grad_gain, m_gain, v_gain, VECTOR_RATE)
    new_shifts, first_shift, second_shift = adamw(shifts, grad_shift, m_shift, v_shift, VECTOR_RATE)
    return (
        out_tokens,
        grad_tokens,
        new_wide,
        new_down,
        new_gains,
        new_shifts,
        first_wide,
        second_wide,
        first_down,
        second_down,
        first_gain,
        second_gain,
        first_shift,
        second_shift,
        low_wide,
        low_down,
    )


def solution(mesh):
    tile = P(("fsdp", "dp"))
    stored = P(None, "fsdp", None)
    in_specs = (tile, tile, tile, tile, P(), stored, stored, P(), P()) + (stored,) * 4 + (P(),) * 4
    out_specs = (tile, tile, stored, stored, P(), P()) + (stored,) * 4 + (P(),) * 4 + (stored,) * 2
    return jax.shard_map(
        on_device, mesh=mesh, in_specs=in_specs, out_specs=out_specs, check_vma=False
    )
```
